32 devices in a mesh: ctx: 8 (over z, x), tp: 4 (over y, core).
Axes of the slice: x: 2, y: 2, z: 4, core: 2. Of those that a mesh axis runs over, the one named last changes fastest.
Arguments:
- inputs: bfloat16 [1024, 4096], P('ctx'), may hold values from -6 to 6
- w_query: bfloat16 [4096, 4096], P(None, 'tp'), may hold values from -0.109375 to 0.109375
- w_key: bfloat16 [4096, 512], P(None, 'tp'), may hold values from -0.109375 to 0.109375
- w_value: bfloat16 [4096, 512], P(None, 'tp'), may hold values from -0.09375 to 0.09375
- attn_out: bfloat16 [1024, 4096], P('ctx', 'tp'), may hold values from -6 to 6
- d_out: bfloat16 [1024, 4096], P('ctx', 'tp'), may hold values from -6 to 6
- block_order: int32 [16], replicated, may hold values from 0 to 15, each once
Outputs:
- d_input: bfloat16 [1024, 4096], P('ctx', 'tp')
The draws below stay inside these ranges and needn't reach their ends.
Inputs may be any that keep to these rules, and one draw needn't show every extreme that they name: `block_order`: a permutation of the sequence blocks.
All inputs are finite; a program needn't handle non-finite values.
Results may differ from the reference program's by a relative error of at most 0.012.
Values may be sent and summed in bfloat16 or wider, within the bound.
A program may use at most 192 MiB of HBM per device.

```python
import jax
import jax.numpy as jnp
from jax import lax

D = 4096
HEADS = 32
KV_HEADS = 4
HD = 128
TOK_DEV = 128
BLOCKS = 16
SEQ = 1024


def draw_w_key(key, part):
    noise = jnp.clip(jax.random.normal(jax.random.fold_in(key, 7102), (D, KV_HEADS * HD), jnp.float32), -6.0, 6.0) * D ** (-0.5)
    return noise.astype(jnp.bfloat16)


def draw_w_query(key, part):
    noise = jnp.clip(jax.random.normal(jax.random.fold_in(key, 7101), (D, HEADS * HD), jnp.float32), -6.0, 6.0) * D ** (-0.5)
    return noise.astype(jnp.bfloat16)


def draw_inputs(key, part):
    field = jnp.clip(jax.random.normal(jax.random.fold_in(key, 7201), (SEQ, D), jnp.float32), -6.0, 6.0)
    return field.astype(jnp.bfloat16)


def shard_levels(stream_key, dims, shards, least, high):
    def one(axis_at, parts):
        heights = jax.random.uniform(jax.random.fold_in(jax.random.fold_in(stream_key, 6), axis_at), (parts,), jnp.float32, least / len(shards), high / len(shards))
        return jnp.repeat(jnp.exp(heights), dims[axis_at] // parts).reshape((-1,) + (1,) * (len(dims) - axis_at - 1))

    level = one(*shards[0])
    for cut in shards[1:]:
        level = level * one(*cut)
    return level


def bell_draw(key, extent, scale, bound, cuts=(), held_as=jnp.bfloat16):
    values = jax.random.normal(key, extent, jnp.float32) * scale
    if len(cuts) > 0:
        values = shard_levels(key, extent, cuts, -0.22, 0.18) * values
    return jnp.clip(values, min=-bound, max=bound).astype(held_as)


def setup_inputs(seed: int = 0) -> dict:
    key_list = jax.random.split(jax.random.key(seed), 8)
    return {
        "inputs": draw_inputs(jax.random.fold_in(key_list[7], 71), 0),
        "w_query": draw_w_query(jax.random.fold_in(key_list[7], 71), 0),
        "w_key": draw_w_key(jax.random.fold_in(key_list[7], 71), 0),
        "w_value": bell_draw(key_list[3], (D, KV_HEADS * HD), D ** -0.5, 0.09375, ((1, 4),)),
        "attn_out": bell_draw(key_list[4], (SEQ, HEADS * HD), 1.0, 6.0, ((0, 8), (1, 4))),
        "d_out": bell_draw(key_list[5], (SEQ, HEADS * HD), 1.0, 6.0, ((0, 8), (1, 4))),
        "block_order": jax.random.permutation(key_list[6], BLOCKS).astype(jnp.int32),
    }


def reference(inputs, w_query, w_key, w_value, attn_out, d_out, block_order):
    seq = inputs.shape[0]
    span = TOK_DEV // 2
    rows = jnp.arange(seq, dtype=jnp.int32)
    pos = block_order[rows // span] * span + rows % span
    scale = HD ** -0.5
    group = HEADS // KV_HEADS
    queries = jnp.dot(inputs, w_query, preferred_element_type=jnp.float32).astype(jnp.bfloat16).reshape(seq, HEADS, HD)
    keys = jnp.dot(inputs, w_key, preferred_element_type=jnp.float32).astype(jnp.bfloat16).reshape(seq, KV_HEADS, HD)
    values = jnp.dot(inputs, w_value, preferred_element_type=jnp.float32).astype(jnp.bfloat16).reshape(seq, KV_HEADS, HD)
    grads3 = d_out.reshape(seq, HEADS, HD)
    outs3 = attn_out.reshape(seq, HEADS, HD)
    delta = jnp.sum(grads3.astype(jnp.float32) * outs3.astype(jnp.float32), axis=-1)
    qblock = min(1024, seq)
    nblock = seq // qblock

    def per_group(g):
        qg = lax.dynamic_slice_in_dim(queries, g * group, group, 1).astype(jnp.float32)
        dg = lax.dynamic_slice_in_dim(grads3, g * group, group, 1).astype(jnp.float32)
        eg = lax.dynamic_slice_in_dim(delta, g * group, group, 1)
        kg = lax.dynamic_index_in_dim(keys, g, 1, keepdims=False).astype(jnp.float32)
        vg = lax.dynamic_index_in_dim(values, g, 1, keepdims=False).astype(jnp.float32)

        def step(carry, b):
            dk, dv = carry
            start = b * qblock
            qs = lax.dynamic_slice_in_dim(qg, start, qblock, 0)
            ds_rows = lax.dynamic_slice_in_dim(dg, start, qblock, 0)
            es = lax.dynamic_slice_in_dim(eg, start, qblock, 0)
            ps = lax.dynamic_slice_in_dim(pos, start, qblock, 0)
            mask = pos[None, :] <= ps[:, None]
            s = jnp.einsum('thd,nd->htn', qs, kg) * scale
            s = jnp.where(mask[None], s, -jnp.inf)
            top = jnp.max(s, axis=-1, keepdims=True)
            lse = top + jnp.log(jnp.sum(jnp.exp(s - top), axis=-1, keepdims=True))
            p = jnp.where(mask[None], jnp.exp(s - lse), 0.0)
            dp = jnp.einsum('thd,nd->htn', ds_rows, vg)
            dsc = p * (dp - es.T[:, :, None])
            ds_b = (dsc * scale).astype(jnp.bfloat16).astype(jnp.float32)
            p_b = p.astype(jnp.bfloat16).astype(jnp.float32)
            dq = jnp.einsum('htn,nd->thd', ds_b, kg)
            dk = dk + jnp.einsum('htn,thd->nd', ds_b, qs)
            dv = dv + jnp.einsum('htn,thd->nd', p_b, ds_rows)
            return (dk, dv), dq

        zero = jnp.zeros((seq, HD), jnp.float32)
        (dk, dv), dq = lax.scan(step, (zero, zero), jnp.arange(nblock, dtype=jnp.int32))
        return dq.reshape(seq, group, HD), dk, dv

    dq, dk, dv = lax.map(per_group, jnp.arange(KV_HEADS, dtype=jnp.int32))
    dq_b = jnp.transpose(dq, (1, 0, 2, 3)).reshape(seq, HEADS * HD).astype(jnp.bfloat16)
    dk_b = jnp.transpose(dk, (1, 0, 2)).reshape(seq, KV_HEADS * HD).astype(jnp.bfloat16)
    dv_b = jnp.transpose(dv, (1, 0, 2)).reshape(seq, KV_HEADS * HD).astype(jnp.bfloat16)
    total = jnp.dot(dq_b, w_query.T, preferred_element_type=jnp.float32)
    total = total + jnp.dot(dk_b, w_key.T, preferred_element_type=jnp.float32)
    total = total + jnp.dot(dv_b, w_value.T, preferred_element_type=jnp.float32)
    return total.astype(jnp.bfloat16)
```

```python
import functools
import math

import jax
import jax.numpy as jnp
from jax import lax
from jax.experimental import pallas as pl
from jax.experimental.pallas import tpu as pltpu
from jax.sharding import PartitionSpec as P

MESH = pl.DeviceIdType.MESH
F32 = jnp.float32
BF16 = jnp.bfloat16
big_negative = -1e30
q_chunks = 4


def dot(a, b):
    return jnp.dot(a, b, preferred_element_type=F32)


def kernel(
    n, m, order, x_hbm, wq_hbm, wk_hbm, wv_hbm, ao_hbm, do_hbm, out,
    x, wq, wkv, ao, do, q_acc, q_rows, q_cols, do_rows, do_cols, delta, top, total,
    kv, p_b, ds_b, dq_cols, part, from_partner, z_out, z_in, dq_b, grads,
    t_out, t_in, y_out, y_in,
    load_sem, wq_sem, kv_send, kv_fwd, kv_recv, part_send, part_recv, z_send, z_recv,
    t_send, t_recv, y_send, y_recv,
):
    tokens, width = x.shape
    head_dim = wk_hbm.shape[1]
    heads = wq.shape[1] // head_dim
    rows = heads * tokens
    span = tokens // 2
    scale = head_dim ** (-0.5)
    scale2 = scale * math.log2(math.e)
    nz, na = n // 2, m // 2
    me, mt = lax.axis_index("ctx"), lax.axis_index("tp")
    z, side = me // 2, lax.rem(me, 2)
    other = 1 - side
    partner = z * 2 + other
    pair, core = mt // 2, lax.rem(mt, 2)
    t_partner = pair * 2 + 1 - core
    features = width // m

    def peer(j):
        return lax.rem(z + j, nz)

    def local(src, dst, sem):
        return pltpu.make_async_copy(src, dst, sem)

    def remote(src, dst, send, recv, axis, to):
        return pltpu.make_async_remote_copy(
            src_ref=src, dst_ref=dst, send_sem=send, recv_sem=recv,
            device_id={axis: to}, device_id_type=MESH,
        )

    loads = [
        local(x_hbm, x, load_sem.at[0]),
        local(wk_hbm, wkv.at[:, pl.ds(0, head_dim)], load_sem.at[1]),
        local(wv_hbm, wkv.at[:, pl.ds(head_dim, head_dim)], load_sem.at[2]),
        local(do_hbm, do, load_sem.at[3]),
        local(ao_hbm, ao, load_sem.at[4]),
    ]
    depth = width // q_chunks
    wq_loads = [
        local(wq_hbm.at[pl.ds(i * depth, depth)], wq.at[pl.ds(i * depth, depth)], wq_sem.at[i])
        for i in range(q_chunks)
    ]
    for copy in loads[:3] + wq_loads + loads[3:]:
        copy.start()

    barrier = pltpu.get_barrier_semaphore()

    def greet(axis, to):
        pl.semaphore_signal(barrier, inc=1, device_id={axis: to}, device_id_type=MESH)

    greet("ctx", partner)
    greet("tp", t_partner)

    def greet_z(j, c):
        greet("ctx", peer(j) * 2 + side)
        return c

    lax.fori_loop(1, nz, greet_z, 0)
    for b in range(1, na):
        greet("tp", lax.rem(pair + b, na) * 2 + core)
    pl.semaphore_wait(barrier, nz + na)

    for copy in loads[:3]:
        copy.wait()
    kv[me] = dot(x[...], wkv[...]).astype(BF16)

    def kv_copy(slot, send, to):
        return remote(kv.at[slot], kv.at[slot], send, kv_recv.at[slot], "ctx", to)

    def kv_out(j):
        return kv_copy(me, kv_send.at[j], peer(j) * 2 + side)

    def forward(j):
        return kv_copy(peer(j) * 2 + side, kv_fwd.at[j], partner)

    def start_out(j, c):
        kv_out(j).start()
        return c

    lax.fori_loop(1, nz, start_out, 0)
    forward(0).start()

    def pass_on(j, c):
        slot = peer(j) * 2 + side
        kv_copy(slot, kv_fwd.at[j], partner).wait_recv()
        forward(j).start()
        return c

    for i in range(q_chunks):
        wq_loads[i].wait()
        piece = dot(x[:, i * depth:(i + 1) * depth], wq[i * depth:(i + 1) * depth, :])
        q_acc[...] = piece if i == 0 else q_acc[...] + piece
    first = min(2, nz)
    lax.fori_loop(1, first, pass_on, 0)
    for h in range(heads):
        r, c = slice(h * tokens, (h + 1) * tokens), slice(h * head_dim, (h + 1) * head_dim)
        q_h = q_acc[:, c]
        q_rows[r, :] = q_h.astype(BF16)
        q_cols[:, r] = q_h.T.astype(BF16)
    second = min(3, nz)
    lax.fori_loop(first, second, pass_on, 0)
    for copy in loads[3:]:
        copy.wait()
    for h in range(heads):
        r, c = slice(h * tokens, (h + 1) * tokens), slice(h * head_dim, (h + 1) * head_dim)
        do_h = do[:, c].astype(F32)
        do_rows[r, :] = do[:, c]
        do_cols[:, r] = do_h.T.astype(BF16)
        delta[:, r] = jnp.sum((do_h * ao[:, c].astype(F32)).T, axis=0, keepdims=True)
    lax.fori_loop(second, nz, pass_on, 0)

    lanes = max(2 * tokens, 256) if heads % 2 == 0 else tokens
    chunks = rows // lanes
    lane = lax.rem(lax.broadcasted_iota(jnp.int32, (1, lanes), 1), tokens)
    o0, o1 = order[me * 2], order[me * 2 + 1]
    query_pos = jnp.where(lane < span, o0 * span + lane, o1 * span + lane - span)
    key_row = lax.broadcasted_iota(jnp.int32, (2 * tokens, 1), 0)

    def allowed(to):
        key_pos = order[to * 4] * span + key_row
        for i in range(1, 4):
            key_pos = jnp.where(
                key_row >= i * span, order[to * 4 + i] * span + key_row - i * span, key_pos
            )
        return key_pos <= query_pos

    def pair_kv(to):
        return kv[pl.ds(to * 2, 2)].reshape(2 * tokens, 2 * head_dim)

    top[...] = jnp.full_like(top, big_negative)
    total[...] = jnp.zeros_like(total)

    def stats(j, carry):
        to = peer(j)
        slot = to * 2 + other
        kv_copy(slot, kv_fwd.at[j], partner).wait_recv()
        mask = allowed(to)
        keys = pair_kv(to)[:, :head_dim]
        for c in range(chunks):
            at = slice(c * lanes, (c + 1) * lanes)
            s = jnp.where(mask, dot(keys, q_cols[:, at]) * scale2, big_negative)
            old = top[:, at]
            new = jnp.maximum(old, jnp.max(s, axis=0, keepdims=True))
            total[:, at] = total[:, at] * jnp.exp2(old - new) + jnp.sum(
                jnp.exp2(s - new), axis=0, keepdims=True
            )
            top[:, at] = new
        return carry

    lax.fori_loop(0, nz, stats, 0)
    top[...] = top[...] + jnp.log(total[...]) * math.log2(math.e)
    dq_cols[...] = jnp.zeros_like(dq_cols)

    def to_partner(j):
        to = peer(j)
        return remote(
            part.at[to, other], from_partner.at[to], part_send.at[j], part_recv.at[j],
            "ctx", partner,
        )

    def to_owner(j):
        to = peer(j)
        return remote(
            z_out.at[j], z_in.at[j], z_send.at[j], z_recv.at[j], "ctx", to * 2 + side
        )

    def settle(j):
        to = peer(j)
        to_partner(j).wait_recv()
        both = part[to, side].astype(F32) + from_partner[to].astype(F32)
        z_out[j] = both.astype(BF16)
        to_owner(j).start()

    def grad(i, carry):
        j = lax.rem(i + 1, nz)
        to = peer(j)
        mask = allowed(to)
        both = pair_kv(to)
        keys, values = both[:, :head_dim], both[:, head_dim:]
        for c in range(chunks):
            at = slice(c * lanes, (c + 1) * lanes)
            s = jnp.where(mask, dot(keys, q_cols[:, at]) * scale2, big_negative)
            p = jnp.exp2(s - top[:, at])
            dp = dot(values, do_cols[:, at])
            p_b[:, at] = p.astype(BF16)
            ds_b[:, at] = (p * (dp - delta[:, at])).astype(BF16)
        dk = dot(ds_b[...], q_rows[...]) * scale
        dv = dot(p_b[...], do_rows[...])
        part[to, :, :, :head_dim] = dk.astype(BF16).reshape(2, tokens, head_dim)
        part[to, :, :, head_dim:] = dv.astype(BF16).reshape(2, tokens, head_dim)
        to_partner(j).start()
        dq_cols[...] += dot(keys.T, ds_b[...])

        @pl.when(i > 0)
        def _():
            settle(i)

        return carry

    lax.fori_loop(0, nz, grad, 0)

    for h in range(heads):
        dq_b[h * head_dim:(h + 1) * head_dim, :] = (
            dq_cols[:, h * tokens:(h + 1) * tokens] * scale
        ).astype(BF16)
    tile = min(512, width)

    def query_terms(i, carry):
        at = pl.ds(pl.multiple_of(i * tile, tile), tile)
        grads[at, :] = dot(wq[at, :], dq_b[...])
        return carry

    lax.fori_loop(0, width // tile, query_terms, 0)

    to_partner(0).wait_recv()
    mine = part[z, side].astype(F32) + from_partner[z].astype(F32)

    def gather_terms(j, acc):
        to_owner(j).wait_recv()
        return acc + z_in[j].astype(F32)

    mine = lax.fori_loop(1, nz, gather_terms, mine)
    dkv = mine.T.astype(BF16)

    def rows_of(b, c):
        start = (lax.rem(pair + b, na) * 2 + c) * features
        return pl.ds(pl.multiple_of(start, features), features)

    def to_core(b):
        return remote(t_out.at[b], t_in.at[b], t_send.at[b], t_recv.at[b], "tp", t_partner)

    def across(b):
        to = lax.rem(pair + b, na) * 2 + core
        return remote(y_out.at[b], y_in.at[b], y_send.at[b], y_recv.at[b], "tp", to)

    turn = [b % na for b in range(1, na + 1)]
    for b in turn:
        at = rows_of(b, 1 - core)
        t_out[b] = (grads[at, :] + dot(wkv[at, :], dkv)).astype(BF16)
        to_core(b).start()
    for b in turn:
        at = rows_of(b, core)
        term = grads[at, :] + dot(wkv[at, :], dkv)
        to_core(b).wait_recv()
        term = term + t_in[b].astype(F32)
        if b > 0:
            y_out[b] = term.astype(BF16)
            across(b).start()
        else:
            grads[at, :] = term
    at = rows_of(0, core)
    term = grads[at, :]
    for b in range(1, na):
        across(b).wait_recv()
        term = term + y_in[b].astype(F32)
    out[...] = term.T.astype(BF16)

    def drain(j, carry):
        forward(j).wait_send()
        to_partner(j).wait_send()
        return carry

    def drain_z(j, carry):
        kv_out(j).wait_send()
        to_owner(j).wait_send()
        return carry

    lax.fori_loop(0, nz, drain, 0)
    lax.fori_loop(1, nz, drain_z, 0)
    for b in range(na):
        to_core(b).wait_send()
        if b > 0:
            across(b).wait_send()


def on_device(n, m, inputs, w_query, w_key, w_value, attn_out, d_out, block_order):
    tokens, width = inputs.shape
    head_dim = w_key.shape[1]
    local_width = w_query.shape[1]
    rows = local_width // head_dim * tokens
    features = width // m
    nz, na = n // 2, m // 2
    vmem, dma = pltpu.VMEM, pltpu.SemaphoreType.DMA
    block = (tokens, 2 * head_dim)
    scratch = [
        vmem((tokens, width), BF16),
        vmem((width, local_width), BF16),
        vmem((width, 2 * head_dim), BF16),
        vmem((tokens, local_width), BF16),
        vmem((tokens, local_width), BF16),
        vmem((tokens, local_width), F32),
        vmem((rows, head_dim), BF16),
        vmem((head_dim, rows), BF16),
        vmem((rows, head_dim), BF16),
        vmem((head_dim, rows), BF16),
        vmem((1, rows), F32),
        vmem((1, rows), F32),
        vmem((1, rows), F32),
        vmem((n, *block), BF16),
        vmem((2 * tokens, rows), BF16),
        vmem((2 * tokens, rows), BF16),
        vmem((head_dim, rows), F32),
        vmem((nz, 2, *block), BF16),
        vmem((nz, *block), BF16),
        vmem((nz, *block), BF16),
        vmem((nz, *block), BF16),
        vmem((local_width, tokens), BF16),
        vmem((width, tokens), F32),
        vmem((na, features, tokens), BF16),
        vmem((na, features, tokens), BF16),
        vmem((na, features, tokens), BF16),
        vmem((na, features, tokens), BF16),
        dma((5,)), dma((q_chunks,)), dma((nz,)), dma((nz,)), dma((n,)),
        dma((nz,)), dma((nz,)), dma((nz,)), dma((nz,)),
        dma((na,)), dma((na,)), dma((na,)), dma((na,)),
    ]
    seq = tokens * n
    flops = 2 * tokens * (2 * width * (local_width + 2 * head_dim) + 6 * seq * local_width)
    return pl.pallas_call(
        functools.partial(kernel, n, m),
        out_shape=jax.ShapeDtypeStruct((tokens, features), BF16),
        in_specs=[pl.BlockSpec(memory_space=pltpu.SMEM)] + [pl.BlockSpec(memory_space=pl.ANY)] * 6,
        out_specs=pl.BlockSpec(memory_space=pltpu.VMEM),
        scratch_shapes=scratch,
        compiler_params=pltpu.CompilerParams(
            collective_id=0, has_side_effects=True, vmem_limit_bytes=58 * 2**20
        ),
        cost_estimate=pl.CostEstimate(
            flops=flops, bytes_accessed=2 * width * (local_width + 2 * head_dim + 2 * tokens),
            transcendentals=2 * rows * seq,
        ),
    )(block_order, inputs, w_query, w_key, w_value, attn_out, d_out)


def solution(mesh):
    placed = (
        P("ctx", None),
        P(None, "tp"),
        P(None, "tp"),
        P(None, "tp"),
        P("ctx", "tp"),
        P("ctx", "tp"),
        P(),
    )
    return jax.shard_map(
        functools.partial(on_device, mesh.shape["ctx"], mesh.shape["tp"]),
        mesh=mesh, in_specs=placed, out_specs=P("ctx", "tp"), check_vma=False,
    )
```

```python
import functools
import math

import jax
import jax.numpy as jnp
from jax import lax
from jax.experimental import pallas as pl
from jax.experimental.pallas import tpu as pltpu
from jax.sharding import PartitionSpec as P

MESH = pl.DeviceIdType.MESH
F32 = jnp.float32
BF16 = jnp.bfloat16
big_negative = -1e30
q_chunks = 4
pieces = 4


def dot(a, b):
    return jnp.dot(a, b, preferred_element_type=F32)


def kernel(
    n, m, order, x_hbm, wq_hbm, wk_hbm, wv_hbm, ao_hbm, do_hbm, out,
    x, wq, wkv, ao, do, q_acc, q_rows, q_cols, do_rows, do_cols, delta, top, total,
    kk, vv, p_b, ds_b, dq_cols, part, from_partner, z_out, z_in, dq_b, grads,
    t_out, t_in, y_out, y_in,
    load_sem, side_sem, kv_send, kv_fwd, kv_recv, part_send, part_recv, z_send, z_recv,
    t_send, t_recv, y_send, y_recv,
):
    tokens, width = x.shape
    head_dim = wk_hbm.shape[1]
    heads = wq.shape[1] // head_dim
    rows = heads * tokens
    span = tokens // 2
    scale = head_dim ** (-0.5)
    scale2 = scale * math.log2(math.e)
    nz, na = n // 2, m // 2
    me, mt = lax.axis_index("ctx"), lax.axis_index("tp")
    z, side = me // 2, lax.rem(me, 2)
    other = 1 - side
    partner = z * 2 + other
    pair, core = mt // 2, lax.rem(mt, 2)
    t_partner = pair * 2 + 1 - core
    features = width // m

    def peer(j):
        return lax.rem(z + j, nz)

    def local(src, dst, sem):
        return pltpu.make_async_copy(src, dst, sem)

    def remote(src, dst, send, recv, axis, to):
        return pltpu.make_async_remote_copy(
            src_ref=src, dst_ref=dst, send_sem=send, recv_sem=recv,
            device_id={axis: to}, device_id_type=MESH,
        )

    depth = width // q_chunks

    steps = [slice(i * depth, (i + 1) * depth) for i in range(q_chunks)]
    down = [pl.ds(i * depth, depth) for i in range(q_chunks)]
    x_loads = [
        local(x_hbm.at[:, d], x.at[:, d], load_sem.at[0, i]) for i, d in enumerate(down)
    ]
    wk_loads = [
        local(wk_hbm.at[d], wkv.at[d, pl.ds(0, head_dim)], load_sem.at[1, i])
        for i, d in enumerate(down)
    ]
    wv_loads = [
        local(wv_hbm.at[d], wkv.at[d, pl.ds(head_dim, head_dim)], load_sem.at[2, i])
        for i, d in enumerate(down)
    ]
    wq_loads = [local(wq_hbm.at[d], wq.at[d], load_sem.at[3, i]) for i, d in enumerate(down)]
    side_loads = [local(do_hbm, do, side_sem.at[0]), local(ao_hbm, ao, side_sem.at[1])]
    for i in range(q_chunks):
        x_loads[i].start()
        wk_loads[i].start()
    for copy in wv_loads:
        copy.start()

    barrier = pltpu.get_barrier_semaphore()

    def greet(axis, to):
        pl.semaphore_signal(barrier, inc=1, device_id={axis: to}, device_id_type=MESH)

    greet("ctx", partner)
    greet("tp", t_partner)

    def greet_z(j, c):
        greet("ctx", peer(j) * 2 + side)
        return c

    lax.fori_loop(1, nz, greet_z, 0)
    for b in range(1, na):
        greet("tp", lax.rem(pair + b, na) * 2 + core)

    def kv_copy(kind, slot, send, to):
        held = (kk, vv)[kind]
        return remote(held.at[slot], held.at[slot], send, kv_recv.at[kind, slot], "ctx", to)

    def kv_out(kind, j):
        return kv_copy(kind, me, kv_send.at[kind, j], peer(j) * 2 + side)

    def forward(kind, j):
        return kv_copy(kind, peer(j) * 2 + side, kv_fwd.at[kind, j], partner)

    def send_own(kind):
        def start_out(j, c):
            kv_out(kind, j).start()
            return c

        lax.fori_loop(1, nz, start_out, 0)
        forward(kind, 0).start()

    def pass_on(kind, j, c):
        forward(kind, j).wait_recv()
        forward(kind, j).start()
        return c

    pass_key = functools.partial(pass_on, 0)

    keys = None
    for i in range(q_chunks):
        x_loads[i].wait()
        wk_loads[i].wait()
        wq_loads[i].start()
        piece = dot(x[:, steps[i]], wkv[steps[i], :head_dim])
        keys = piece if i == 0 else keys + piece
    kk[me] = keys.astype(BF16)
    pl.semaphore_wait(barrier, nz + na)
    send_own(0)
    for copy in side_loads:
        copy.start()
    for copy in wv_loads:
        copy.wait()
    vv[me] = dot(x[...], wkv[:, head_dim:]).astype(BF16)
    send_own(1)

    for i in range(q_chunks):
        wq_loads[i].wait()
        piece = dot(x[:, steps[i]], wq[steps[i], :])
        q_acc[...] = piece if i == 0 else q_acc[...] + piece
    first = min(2, nz)
    lax.fori_loop(1, first, pass_key, 0)
    for h in range(heads):
        r, c = slice(h * tokens, (h + 1) * tokens), slice(h * head_dim, (h + 1) * head_dim)
        q_h = q_acc[:, c].astype(BF16)
        q_rows[r, :] = q_h
        q_cols[:, r] = q_h.T
    second = min(3, nz)
    lax.fori_loop(first, second, pass_key, 0)
    for copy in side_loads:
        copy.wait()
    for h in range(heads):
        r, c = slice(h * tokens, (h + 1) * tokens), slice(h * head_dim, (h + 1) * head_dim)
        do_h = do[:, c]
        do_rows[r, :] = do_h
        do_cols[:, r] = do_h.T
        both = do_h.astype(F32) * ao[:, c].astype(F32)
        delta[:, r] = jnp.sum(both.T, axis=0, keepdims=True)
    lax.fori_loop(second, nz, pass_key, 0)

    lanes = max(2 * tokens, 256) if heads % 2 == 0 else tokens
    chunks = rows // lanes
    lane = lax.rem(lax.broadcasted_iota(jnp.int32, (1, lanes), 1), tokens)
    o0, o1 = order[me * 2], order[me * 2 + 1]
    query_pos = jnp.where(lane < span, o0 * span + lane, o1 * span + lane - span)
    key_row = lax.broadcasted_iota(jnp.int32, (2 * tokens, 1), 0)

    def allowed(to):
        key_pos = order[to * 4] * span + key_row
        for i in range(1, 4):
            key_pos = jnp.where(
                key_row >= i * span, order[to * 4 + i] * span + key_row - i * span, key_pos
            )
        return key_pos <= query_pos

    def pair_of(held, to):
        return held[pl.ds(to * 2, 2)].reshape(2 * tokens, head_dim)

    top[...] = jnp.full_like(top, big_negative)
    total[...] = jnp.zeros_like(total)

    def stats(j, carry):
        to = peer(j)
        kv_copy(0, to * 2 + other, kv_fwd.at[0, j], partner).wait_recv()
        mask = allowed(to)
        keys = pair_of(kk, to)
        for c in range(chunks):
            at = slice(c * lanes, (c + 1) * lanes)
            s = jnp.where(mask, dot(keys, q_cols[:, at]) * scale2, big_negative)
            old = top[:, at]
            new = jnp.maximum(old, jnp.max(s, axis=0, keepdims=True))
            total[:, at] = total[:, at] * jnp.exp2(old - new) + jnp.sum(
                jnp.exp2(s - new), axis=0, keepdims=True
            )
            top[:, at] = new

        @pl.when(j + 1 < nz)
        def _():
            pass_on(1, j + 1, 0)

        return carry

    lax.fori_loop(0, nz, stats, 0)
    top[...] = top[...] + jnp.log(total[...]) * math.log2(math.e)
    dq_cols[...] = jnp.zeros_like(dq_cols)

    def to_partner(j):
        to = peer(j)
        return remote(
            part.at[to, other], from_partner.at[to], part_send.at[j], part_recv.at[j],
            "ctx", partner,
        )

    def to_owner(j):
        to = peer(j)
        return remote(
            z_out.at[j], z_in.at[j], z_send.at[j], z_recv.at[j], "ctx", to * 2 + side
        )

    def settle(j):
        to = peer(j)
        to_partner(j).wait_recv()
        both = part[to, side].astype(F32) + from_partner[to].astype(F32)
        z_out[j] = both.astype(BF16)
        to_owner(j).start()

    def grad(i, carry):
        j = lax.rem(i + 1, nz)
        to = peer(j)
        mask = allowed(to)
        kv_copy(1, to * 2 + other, kv_fwd.at[1, j], partner).wait_recv()
        keys, values = pair_of(kk, to), pair_of(vv, to)
        for c in range(chunks):
            at = slice(c * lanes, (c + 1) * lanes)
            s = jnp.where(mask, dot(keys, q_cols[:, at]) * scale2, big_negative)
            p = jnp.exp2(s - top[:, at])
            dp = dot(values, do_cols[:, at])
            p_b[:, at] = p.astype(BF16)
            ds_b[:, at] = (p * (dp - delta[:, at])).astype(BF16)
        dk = dot(ds_b[...], q_rows[...]) * scale
        dv = dot(p_b[...], do_rows[...])
        part[to, :, :, :head_dim] = dk.astype(BF16).reshape(2, tokens, head_dim)
        part[to, :, :, head_dim:] = dv.astype(BF16).reshape(2, tokens, head_dim)
        to_partner(j).start()
        dq_cols[...] += dot(keys.T, ds_b[...])

        @pl.when(i > 1)
        def _():
            settle(i - 1)

        return carry

    lax.fori_loop(0, nz, grad, 0)

    for h in range(heads):
        dq_b[h * head_dim:(h + 1) * head_dim, :] = (
            dq_cols[:, h * tokens:(h + 1) * tokens] * scale
        ).astype(BF16)
    tile = min(512, width)

    def query_terms(i, carry):
        at = pl.ds(pl.multiple_of(i * tile, tile), tile)
        grads[at, :] = dot(wq[at, :], dq_b[...])
        return carry

    early = max(1, width // tile // 4)
    lax.fori_loop(0, early, query_terms, 0)
    if nz > 1:
        settle(nz - 1)
    lax.fori_loop(early, width // tile, query_terms, 0)

    to_partner(0).wait_recv()
    mine = part[z, side].astype(F32) + from_partner[z].astype(F32)

    def gather_terms(j, acc):
        to_owner(j).wait_recv()
        return acc + z_in[j].astype(F32)

    mine = lax.fori_loop(1, nz, gather_terms, mine)
    dkv = mine.T.astype(BF16)

    size = features // pieces

    def rows_of(b, c, i):
        start = (lax.rem(pair + b, na) * 2 + c) * features + i * size
        return pl.ds(pl.multiple_of(start, size), size)

    def to_core(b, i):
        return remote(
            t_out.at[b, i], t_in.at[b, i], t_send.at[b, i], t_recv.at[b, i], "tp", t_partner
        )

    def across(b, i):
        to = lax.rem(pair + b, na) * 2 + core
        return remote(y_out.at[b, i], y_in.at[b, i], y_send.at[b, i], y_recv.at[b, i], "tp", to)

    for b in [b % na for b in range(1, na + 1)]:
        for i in range(pieces):
            at = rows_of(b, 1 - core, i)
            t_out[b, i] = (grads[at, :] + dot(wkv[at, :], dkv)).astype(BF16)
            to_core(b, i).start()
        for i in range(pieces):
            at = rows_of(b, core, i)
            term = grads[at, :] + dot(wkv[at, :], dkv)
            to_core(b, i).wait_recv()
            term = term + t_in[b, i].astype(F32)
            if b > 0:
                y_out[b, i] = term.astype(BF16)
                across(b, i).start()
            else:
                grads[at, :] = term
    for i in range(pieces):
        term = grads[rows_of(0, core, i), :]
        for b in range(1, na):
            across(b, i).wait_recv()
            term = term + y_in[b, i].astype(F32)
        out[:, i * size:(i + 1) * size] = term.T.astype(BF16)

    def drain(j, carry):
        forward(0, j).wait_send()
        forward(1, j).wait_send()
        to_partner(j).wait_send()
        return carry

    def drain_z(j, carry):
        kv_out(0, j).wait_send()
        kv_out(1, j).wait_send()
        to_owner(j).wait_send()
        return carry

    lax.fori_loop(0, nz, drain, 0)
    lax.fori_loop(1, nz, drain_z, 0)
    for b in range(na):
        for i in range(pieces):
            to_core(b, i).wait_send()
            if b > 0:
                across(b, i).wait_send()


def on_device(n, m, inputs, w_query, w_key, w_value, attn_out, d_out, block_order):
    tokens, width = inputs.shape
    head_dim = w_key.shape[1]
    local_width = w_query.shape[1]
    rows = local_width // head_dim * tokens
    features = width // m
    nz, na = n // 2, m // 2
    vmem, dma = pltpu.VMEM, pltpu.SemaphoreType.DMA
    block = (tokens, 2 * head_dim)
    scratch = [
        vmem((tokens, width), BF16),
        vmem((width, local_width), BF16),
        vmem((width, 2 * head_dim), BF16),
        vmem((tokens, local_width), BF16),
        vmem((tokens, local_width), BF16),
        vmem((tokens, local_width), F32),
        vmem((rows, head_dim), BF16),
        vmem((head_dim, rows), BF16),
        vmem((rows, head_dim), BF16),
        vmem((head_dim, rows), BF16),
        vmem((1, rows), F32),
        vmem((1, rows), F32),
        vmem((1, rows), F32),
        vmem((n, tokens, head_dim), BF16),
        vmem((n, tokens, head_dim), BF16),
        vmem((2 * tokens, rows), BF16),
        vmem((2 * tokens, rows), BF16),
        vmem((head_dim, rows), F32),
        vmem((nz, 2, *block), BF16),
        vmem((nz, *block), BF16),
        vmem((nz, *block), BF16),
        vmem((nz, *block), BF16),
        vmem((local_width, tokens), BF16),
        vmem((width, tokens), F32),
        vmem((na, pieces, features // pieces, tokens), BF16),
        vmem((na, pieces, features // pieces, tokens), BF16),
        vmem((na, pieces, features // pieces, tokens), BF16),
        vmem((na, pieces, features // pieces, tokens), BF16),
        dma((4, q_chunks)), dma((2,)), dma((2, nz)), dma((2, nz)), dma((2, n)),
        dma((nz,)), dma((nz,)), dma((nz,)), dma((nz,)),
        dma((na, pieces)), dma((na, pieces)), dma((na, pieces)), dma((na, pieces)),
    ]
    seq = tokens * n
    flops = 2 * tokens * (2 * width * (local_width + 2 * head_dim) + 6 * seq * local_width)
    return pl.pallas_call(
        functools.partial(kernel, n, m),
        out_shape=jax.ShapeDtypeStruct((tokens, features), BF16),
        in_specs=[pl.BlockSpec(memory_space=pltpu.SMEM)] + [pl.BlockSpec(memory_space=pl.ANY)] * 6,
        out_specs=pl.BlockSpec(memory_space=pltpu.VMEM),
        scratch_shapes=scratch,
        compiler_params=pltpu.CompilerParams(
            collective_id=0, has_side_effects=True, vmem_limit_bytes=58 * 2**20
        ),
        cost_estimate=pl.CostEstimate(
            flops=flops, bytes_accessed=2 * width * (local_width + 2 * head_dim + 2 * tokens),
            transcendentals=2 * rows * seq,
        ),
    )(block_order, inputs, w_query, w_key, w_value, attn_out, d_out)


def solution(mesh):
    placed = (
        P("ctx", None),
        P(None, "tp"),
        P(None, "tp"),
        P(None, "tp"),
        P("ctx", "tp"),
        P("ctx", "tp"),
        P(),
    )
    return jax.shard_map(
        functools.partial(on_device, mesh.shape["ctx"], mesh.shape["tp"]),
        mesh=mesh, in_specs=placed, out_specs=P("ctx", "tp"), check_vma=False,
    )
```

```python
import functools
import math

import jax
import jax.numpy as jnp
from jax import lax
from jax.experimental import pallas as pl
from jax.experimental.pallas import tpu as pltpu
from jax.sharding import PartitionSpec as P

MESH = pl.DeviceIdType.MESH
F32 = jnp.float32
BF16 = jnp.bfloat16
big_negative = -1e30
q_chunks = 4
pieces = 4
kept_scores = 8 * 2**20


def dot(a, b):
    return jnp.dot(a, b, preferred_element_type=F32)


def kernel(
    n, m, order, x_hbm, wq_hbm, wk_hbm, wv_hbm, ao_hbm, do_hbm, out,
    x, wq, wkv, ao, do, q_acc, q_rows, q_cols, do_rows, do_cols, delta, top, total,
    kk, vv, scores, dq_cols, part, from_partner, z_out, z_in, dq_b, grads,
    t_out, t_in, y_out, y_in,
    load_sem, side_sem, kv_send, kv_fwd, kv_recv, part_send, part_recv, z_send, z_recv,
    t_send, t_recv, y_send, y_recv,
):
    tokens, width = x.shape
    head_dim = wk_hbm.shape[1]
    heads = wq.shape[1] // head_dim
    rows = heads * tokens
    span = tokens // 2
    scale = head_dim ** (-0.5)
    scale2 = scale * math.log2(math.e)
    nz, na = n // 2, m // 2
    me, mt = lax.axis_index("ctx"), lax.axis_index("tp")
    z, side = me // 2, lax.rem(me, 2)
    other = 1 - side
    partner = z * 2 + other
    pair, core = mt // 2, lax.rem(mt, 2)
    t_partner = pair * 2 + 1 - core
    features = width // m

    def peer(j):
        return lax.rem(z + j, nz)

    def local(src, dst, sem):
        return pltpu.make_async_copy(src, dst, sem)

    def remote(src, dst, send, recv, axis, to):
        return pltpu.make_async_remote_copy(
            src_ref=src, dst_ref=dst, send_sem=send, recv_sem=recv,
            device_id={axis: to}, device_id_type=MESH,
        )

    depth = width // q_chunks

    steps = [slice(i * depth, (i + 1) * depth) for i in range(q_chunks)]
    down = [pl.ds(i * depth, depth) for i in range(q_chunks)]
    x_loads = [
        local(x_hbm.at[:, d], x.at[:, d], load_sem.at[0, i]) for i, d in enumerate(down)
    ]
    wk_loads = [
        local(wk_hbm.at[d], wkv.at[d, pl.ds(0, head_dim)], load_sem.at[1, i])
        for i, d in enumerate(down)
    ]
    wv_loads = [
        local(wv_hbm.at[d], wkv.at[d, pl.ds(head_dim, head_dim)], load_sem.at[2, i])
        for i, d in enumerate(down)
    ]
    wq_loads = [local(wq_hbm.at[d], wq.at[d], load_sem.at[3, i]) for i, d in enumerate(down)]
    side_loads = [local(do_hbm, do, side_sem.at[0]), local(ao_hbm, ao, side_sem.at[1])]
    for i in range(q_chunks):
        x_loads[i].start()
        wk_loads[i].start()
    for copy in wv_loads + side_loads:
        copy.start()

    barrier = pltpu.get_barrier_semaphore()

    def greet(axis, to):
        pl.semaphore_signal(barrier, inc=1, device_id={axis: to}, device_id_type=MESH)

    greet("ctx", partner)
    greet("tp", t_partner)

    def greet_z(j, c):
        greet("ctx", peer(j) * 2 + side)
        return c

    lax.fori_loop(1, nz, greet_z, 0)
    for b in range(1, na):
        greet("tp", lax.rem(pair + b, na) * 2 + core)

    def kv_copy(kind, slot, send, to):
        held = (kk, vv)[kind]
        return remote(held.at[slot], held.at[slot], send, kv_recv.at[kind, slot], "ctx", to)

    def kv_out(kind, j):
        return kv_copy(kind, me, kv_send.at[kind, j], peer(j) * 2 + side)

    def forward(kind, j):
        return kv_copy(kind, peer(j) * 2 + side, kv_fwd.at[kind, j], partner)

    def send_own(kind):
        def start_out(j, c):
            kv_out(kind, j).start()
            return c

        lax.fori_loop(1, nz, start_out, 0)
        forward(kind, 0).start()

    def pass_on(kind, j, c):
        forward(kind, j).wait_recv()
        forward(kind, j).start()
        return c

    pass_key = functools.partial(pass_on, 0)

    keys = None
    for i in range(q_chunks):
        x_loads[i].wait()
        wk_loads[i].wait()
        wq_loads[i].start()
        piece = dot(x[:, steps[i]], wkv[steps[i], :head_dim])
        keys = piece if i == 0 else keys + piece
    kk[me] = keys.astype(BF16)
    pl.semaphore_wait(barrier, nz + na)
    send_own(0)
    for copy in wv_loads:
        copy.wait()
    vv[me] = dot(x[...], wkv[:, head_dim:]).astype(BF16)
    send_own(1)

    for copy in side_loads:
        copy.wait()
    for h in range(heads):
        r, c = slice(h * tokens, (h + 1) * tokens), slice(h * head_dim, (h + 1) * head_dim)
        do_h = do[:, c]
        do_rows[r, :] = do_h
        do_cols[:, r] = do_h.T
        both = do_h.astype(F32) * ao[:, c].astype(F32)
        delta[:, r] = jnp.sum(both.T, axis=0, keepdims=True)

    for i in range(q_chunks):
        wq_loads[i].wait()
        piece = dot(x[:, steps[i]], wq[steps[i], :])
        q_acc[...] = piece if i == 0 else q_acc[...] + piece
    first = min(2, nz)
    lax.fori_loop(1, first, pass_key, 0)
    for h in range(heads):
        r, c = slice(h * tokens, (h + 1) * tokens), slice(h * head_dim, (h + 1) * head_dim)
        q_h = q_acc[:, c].astype(BF16)
        q_rows[r, :] = q_h
        q_cols[:, r] = q_h.T
    lax.fori_loop(first, nz, pass_key, 0)

    lanes = max(2 * tokens, 256) if heads % 2 == 0 else tokens
    chunks = rows // lanes
    lane = lax.rem(lax.broadcasted_iota(jnp.int32, (1, lanes), 1), tokens)
    o0, o1 = order[me * 2], order[me * 2 + 1]
    query_pos = jnp.where(lane < span, o0 * span + lane, o1 * span + lane - span)
    key_row = lax.broadcasted_iota(jnp.int32, (2 * tokens, 1), 0)

    def allowed(to):
        key_pos = order[to * 4] * span + key_row
        for i in range(1, 4):
            key_pos = jnp.where(
                key_row >= i * span, order[to * 4 + i] * span + key_row - i * span, key_pos
            )
        return key_pos <= query_pos

    def pair_of(held, to):
        return held[pl.ds(to * 2, 2)].reshape(2 * tokens, head_dim)

    keep = scores.shape[0] == nz
    top[...] = jnp.full_like(top, big_negative)
    total[...] = jnp.zeros_like(total)

    def stats(j, carry):
        to = peer(j)
        kv_copy(0, to * 2 + other, kv_fwd.at[0, j], partner).wait_recv()
        mask = allowed(to)
        keys = pair_of(kk, to)
        for c in range(chunks):
            at = slice(c * lanes, (c + 1) * lanes)
            s = jnp.where(mask, dot(keys, q_cols[:, at]) * scale2, big_negative)
            if keep:
                scores[j, :, at] = s
            old = top[:, at]
            new = jnp.maximum(old, jnp.max(s, axis=0, keepdims=True))
            total[:, at] = total[:, at] * jnp.exp2(old - new) + jnp.sum(
                jnp.exp2(s - new), axis=0, keepdims=True
            )
            top[:, at] = new

        @pl.when(j + 1 < nz)
        def _():
            pass_on(1, j + 1, 0)

        return carry

    lax.fori_loop(0, nz, stats, 0)
    top[...] = top[...] + jnp.log(total[...]) * math.log2(math.e)
    dq_cols[...] = jnp.zeros_like(dq_cols)

    def to_partner(j):
        to = peer(j)
        return remote(
            part.at[to, other], from_partner.at[to], part_send.at[j], part_recv.at[j],
            "ctx", partner,
        )

    def to_owner(j):
        to = peer(j)
        return remote(
            z_out.at[j], z_in.at[j], z_send.at[j], z_recv.at[j], "ctx", to * 2 + side
        )

    def settle(j):
        to = peer(j)
        to_partner(j).wait_recv()
        both = part[to, side].astype(F32) + from_partner[to].astype(F32)
        z_out[j] = both.astype(BF16)
        to_owner(j).start()

    def grad(i, carry):
        j = lax.rem(i + 1, nz)
        to = peer(j)
        mask = None if keep else allowed(to)
        kv_copy(1, to * 2 + other, kv_fwd.at[1, j], partner).wait_recv()
        keys, values = pair_of(kk, to), pair_of(vv, to)
        keys_t = keys.T
        dk = dv = None
        for c in range(chunks):
            at = slice(c * lanes, (c + 1) * lanes)
            if keep:
                s = scores[j, :, at]
            else:
                s = jnp.where(mask, dot(keys, q_cols[:, at]) * scale2, big_negative)
            p = jnp.exp2(s - top[:, at])
            dp = dot(values, do_cols[:, at])
            ds = (p * (dp - delta[:, at])).astype(BF16)
            dv_c, dk_c = dot(p.astype(BF16), do_rows[at, :]), dot(ds, q_rows[at, :])
            dv, dk = (dv_c, dk_c) if c == 0 else (dv + dv_c, dk + dk_c)
            dq_cols[:, at] += dot(keys_t, ds)
        dk = dk * scale
        part[to, :, :, :head_dim] = dk.astype(BF16).reshape(2, tokens, head_dim)
        part[to, :, :, head_dim:] = dv.astype(BF16).reshape(2, tokens, head_dim)
        to_partner(j).start()

        @pl.when(i > 1)
        def _():
            settle(i - 1)

        return carry

    lax.fori_loop(0, nz, grad, 0)

    for h in range(heads):
        dq_b[h * head_dim:(h + 1) * head_dim, :] = (
            dq_cols[:, h * tokens:(h + 1) * tokens] * scale
        ).astype(BF16)
    tile = min(512, width)

    def query_terms(i, carry):
        at = pl.ds(pl.multiple_of(i * tile, tile), tile)
        grads[at, :] = dot(wq[at, :], dq_b[...])
        return carry

    early = max(1, width // tile // 4)
    lax.fori_loop(0, early, query_terms, 0)
    if nz > 1:
        settle(nz - 1)
    lax.fori_loop(early, width // tile, query_terms, 0)

    to_partner(0).wait_recv()
    mine = part[z, side].astype(F32) + from_partner[z].astype(F32)

    def gather_terms(j, acc):
        to_owner(j).wait_recv()
        return acc + z_in[j].astype(F32)

    mine = lax.fori_loop(1, nz, gather_terms, mine)
    dkv = mine.T.astype(BF16)

    size = features // pieces

    def rows_of(b, c, i):
        start = (lax.rem(pair + b, na) * 2 + c) * features + i * size
        return pl.ds(pl.multiple_of(start, size), size)

    def to_core(b, i):
        return remote(
            t_out.at[b, i], t_in.at[b, i], t_send.at[b, i], t_recv.at[b, i], "tp", t_partner
        )

    def across(b, i):
        to = lax.rem(pair + b, na) * 2 + core
        return remote(y_out.at[b, i], y_in.at[b, i], y_send.at[b, i], y_recv.at[b, i], "tp", to)

    for b in [b % na for b in range(1, na + 1)]:
        for i in range(pieces):
            at = rows_of(b, 1 - core, i)
            t_out[b, i] = (grads[at, :] + dot(wkv[at, :], dkv)).astype(BF16)
            to_core(b, i).start()
        for i in range(pieces):
            at = rows_of(b, core, i)
            term = grads[at, :] + dot(wkv[at, :], dkv)
            to_core(b, i).wait_recv()
            term = term + t_in[b, i].astype(F32)
            if b > 0:
                y_out[b, i] = term.astype(BF16)
                across(b, i).start()
            else:
                grads[at, :] = term
    for i in range(pieces):
        term = grads[rows_of(0, core, i), :]
        for b in range(1, na):
            across(b, i).wait_recv()
            term = term + y_in[b, i].astype(F32)
        out[:, i * size:(i + 1) * size] = term.T.astype(BF16)

    def drain(j, carry):
        forward(0, j).wait_send()
        forward(1, j).wait_send()
        to_partner(j).wait_send()
        return carry

    def drain_z(j, carry):
        kv_out(0, j).wait_send()
        kv_out(1, j).wait_send()
        to_owner(j).wait_send()
        return carry

    lax.fori_loop(0, nz, drain, 0)
    lax.fori_loop(1, nz, drain_z, 0)
    for b in range(na):
        for i in range(pieces):
            to_core(b, i).wait_send()
            if b > 0:
                across(b, i).wait_send()


def on_device(n, m, inputs, w_query, w_key, w_value, attn_out, d_out, block_order):
    tokens, width = inputs.shape
    head_dim = w_key.shape[1]
    local_width = w_query.shape[1]
    rows = local_width // head_dim * tokens
    features = width // m
    nz, na = n // 2, m // 2
    keep = n * tokens * rows * 4 <= kept_scores
    vmem, dma = pltpu.VMEM, pltpu.SemaphoreType.DMA
    block = (tokens, 2 * head_dim)
    scratch = [
        vmem((tokens, width), BF16),
        vmem((width, local_width), BF16),
        vmem((width, 2 * head_dim), BF16),
        vmem((tokens, local_width), BF16),
        vmem((tokens, local_width), BF16),
        vmem((tokens, local_width), F32),
        vmem((rows, head_dim), BF16),
        vmem((head_dim, rows), BF16),
        vmem((rows, head_dim), BF16),
        vmem((head_dim, rows), BF16),
        vmem((1, rows), F32),
        vmem((1, rows), F32),
        vmem((1, rows), F32),
        vmem((n, tokens, head_dim), BF16),
        vmem((n, tokens, head_dim), BF16),
        vmem((nz if keep else 1, 2 * tokens, rows), F32),
        vmem((head_dim, rows), F32),
        vmem((nz, 2, *block), BF16),
        vmem((nz, *block), BF16),
        vmem((nz, *block), BF16),
        vmem((nz, *block), BF16),
        vmem((local_width, tokens), BF16),
        vmem((width, tokens), F32),
        vmem((na, pieces, features // pieces, tokens), BF16),
        vmem((na, pieces, features // pieces, tokens), BF16),
        vmem((na, pieces, features // pieces, tokens), BF16),
        vmem((na, pieces, features // pieces, tokens), BF16),
        dma((4, q_chunks)), dma((2,)), dma((2, nz)), dma((2, nz)), dma((2, n)),
        dma((nz,)), dma((nz,)), dma((nz,)), dma((nz,)),
        dma((na, pieces)), dma((na, pieces)), dma((na, pieces)), dma((na, pieces)),
    ]
    seq = tokens * n
    flops = 2 * tokens * (2 * width * (local_width + 2 * head_dim) + 6 * seq * local_width)
    return pl.pallas_call(
        functools.partial(kernel, n, m),
        out_shape=jax.ShapeDtypeStruct((tokens, features), BF16),
        in_specs=[pl.BlockSpec(memory_space=pltpu.SMEM)] + [pl.BlockSpec(memory_space=pl.ANY)] * 6,
        out_specs=pl.BlockSpec(memory_space=pltpu.VMEM),
        scratch_shapes=scratch,
        compiler_params=pltpu.CompilerParams(
            collective_id=0, has_side_effects=True, vmem_limit_bytes=58 * 2**20
        ),
        cost_estimate=pl.CostEstimate(
            flops=flops, bytes_accessed=2 * width * (local_width + 2 * head_dim + 2 * tokens),
            transcendentals=2 * rows * seq,
        ),
    )(block_order, inputs, w_query, w_key, w_value, attn_out, d_out)


def solution(mesh):
    placed = (
        P("ctx", None),
        P(None, "tp"),
        P(None, "tp"),
        P(None, "tp"),
        P("ctx", "tp"),
        P("ctx", "tp"),
        P(),
    )
    return jax.shard_map(
        functools.partial(on_device, mesh.shape["ctx"], mesh.shape["tp"]),
        mesh=mesh, in_specs=placed, out_specs=P("ctx", "tp"), check_vma=False,
    )
```

```python
import functools
import math

import jax
import jax.numpy as jnp
from jax import lax
from jax.experimental import pallas as pl
from jax.experimental.pallas import tpu as pltpu
from jax.sharding import PartitionSpec as P

MESH = pl.DeviceIdType.MESH
F32 = jnp.float32
BF16 = jnp.bfloat16
big_negative = -1e30
q_chunks = 4
pieces = 4
kept_scores = 8 * 2**20


def dot(a, b):
    return jnp.dot(a, b, preferred_element_type=F32)


def kernel(
    n, m, order, x_hbm, wq_hbm, wk_hbm, wv_hbm, ao_hbm, do_hbm, out,
    x, wq, wkv, ao, do, q_acc, q_rows, q_cols, do_rows, do_cols, delta, top, total,
    kk, vv, scores, p_b, ds_b, dq_cols, part, from_partner, z_out, z_in, dq_b, grads,
    t_out, t_in, y_out, y_in,
    load_sem, side_sem, kv_send, kv_fwd, kv_recv, part_send, part_recv, z_send, z_recv,
    t_send, t_recv, y_send, y_recv,
):
    tokens, width = x.shape
    head_dim = wk_hbm.shape[1]
    heads = wq.shape[1] // head_dim
    rows = heads * tokens
    span = tokens // 2
    scale = head_dim ** (-0.5)
    scale2 = scale * math.log2(math.e)
    nz, na = n // 2, m // 2
    me, mt = lax.axis_index("ctx"), lax.axis_index("tp")
    z, side = me // 2, lax.rem(me, 2)
    other = 1 - side
    partner = z * 2 + other
    pair, core = mt // 2, lax.rem(mt, 2)
    t_partner = pair * 2 + 1 - core
    features = width // m

    def peer(j):
        return lax.rem(z + j, nz)

    def local(src, dst, sem):
        return pltpu.make_async_copy(src, dst, sem)

    def remote(src, dst, send, recv, axis, to):
        return pltpu.make_async_remote_copy(
            src_ref=src, dst_ref=dst, send_sem=send, recv_sem=recv,
            device_id={axis: to}, device_id_type=MESH,
        )

    depth = width // q_chunks

    steps = [slice(i * depth, (i + 1) * depth) for i in range(q_chunks)]
    down = [pl.ds(i * depth, depth) for i in range(q_chunks)]
    x_loads = [
        local(x_hbm.at[:, d], x.at[:, d], load_sem.at[0, i]) for i, d in enumerate(down)
    ]
    wk_loads = [
        local(wk_hbm.at[d], wkv.at[d, pl.ds(0, head_dim)], load_sem.at[1, i])
        for i, d in enumerate(down)
    ]
    wv_loads = [
        local(wv_hbm.at[d], wkv.at[d, pl.ds(head_dim, head_dim)], load_sem.at[2, i])
        for i, d in enumerate(down)
    ]
    wq_loads = [local(wq_hbm.at[d], wq.at[d], load_sem.at[3, i]) for i, d in enumerate(down)]
    side_loads = [local(do_hbm, do, side_sem.at[0]), local(ao_hbm, ao, side_sem.at[1])]
    for i in range(q_chunks):
        x_loads[i].start()
        wk_loads[i].start()
    for copy in wv_loads + side_loads:
        copy.start()

    barrier = pltpu.get_barrier_semaphore()

    def greet(axis, to):
        pl.semaphore_signal(barrier, inc=1, device_id={axis: to}, device_id_type=MESH)

    greet("ctx", partner)
    greet("tp", t_partner)

    def greet_z(j, c):
        greet("ctx", peer(j) * 2 + side)
        return c

    lax.fori_loop(1, nz, greet_z, 0)
    for b in range(1, na):
        greet("tp", lax.rem(pair + b, na) * 2 + core)

    def kv_copy(kind, slot, send, to):
        held = (kk, vv)[kind]
        return remote(held.at[slot], held.at[slot], send, kv_recv.at[kind, slot], "ctx", to)

    def kv_out(kind, j):
        return kv_copy(kind, me, kv_send.at[kind, j], peer(j) * 2 + side)

    def forward(kind, j):
        return kv_copy(kind, peer(j) * 2 + side, kv_fwd.at[kind, j], partner)

    def send_own(kind):
        def start_out(j, c):
            kv_out(kind, j).start()
            return c

        lax.fori_loop(1, nz, start_out, 0)
        forward(kind, 0).start()

    def pass_on(kind, j, c):
        forward(kind, j).wait_recv()
        forward(kind, j).start()
        return c

    pass_key = functools.partial(pass_on, 0)

    keys = None
    for i in range(q_chunks):
        x_loads[i].wait()
        wk_loads[i].wait()
        wq_loads[i].start()
        piece = dot(x[:, steps[i]], wkv[steps[i], :head_dim])
        keys = piece if i == 0 else keys + piece
    kk[me] = keys.astype(BF16)
    pl.semaphore_wait(barrier, nz + na)
    send_own(0)
    for copy in wv_loads:
        copy.wait()
    vv[me] = dot(x[...], wkv[:, head_dim:]).astype(BF16)
    send_own(1)

    for copy in side_loads:
        copy.wait()
    for h in range(heads):
        r, c = slice(h * tokens, (h + 1) * tokens), slice(h * head_dim, (h + 1) * head_dim)
        do_h = do[:, c]
        do_rows[r, :] = do_h
        do_cols[:, r] = do_h.T
        both = do_h.astype(F32) * ao[:, c].astype(F32)
        delta[:, r] = jnp.sum(both.T, axis=0, keepdims=True)

    for i in range(q_chunks):
        wq_loads[i].wait()
        piece = dot(x[:, steps[i]], wq[steps[i], :])
        q_acc[...] = piece if i == 0 else q_acc[...] + piece
        last = nz if i == q_chunks - 2 else min(i + 2, nz)
        if i < q_chunks - 1:
            lax.fori_loop(min(i + 1, nz), last, pass_key, 0)
    for h in range(heads):
        r, c = slice(h * tokens, (h + 1) * tokens), slice(h * head_dim, (h + 1) * head_dim)
        q_h = q_acc[:, c].astype(BF16)
        q_rows[r, :] = q_h
        q_cols[:, r] = q_h.T

    lanes = max(2 * tokens, 256) if heads % 2 == 0 else tokens
    chunks = rows // lanes
    lane = lax.rem(lax.broadcasted_iota(jnp.int32, (1, lanes), 1), tokens)
    o0, o1 = order[me * 2], order[me * 2 + 1]
    query_pos = jnp.where(lane < span, o0 * span + lane, o1 * span + lane - span)
    key_row = lax.broadcasted_iota(jnp.int32, (2 * tokens, 1), 0)

    def allowed(to):
        key_pos = order[to * 4] * span + key_row
        for i in range(1, 4):
            key_pos = jnp.where(
                key_row >= i * span, order[to * 4 + i] * span + key_row - i * span, key_pos
            )
        return key_pos <= query_pos

    def pair_of(held, to):
        return held[pl.ds(to * 2, 2)].reshape(2 * tokens, head_dim)

    keep = scores.shape[0] == nz
    top[...] = jnp.full_like(top, big_negative)
    total[...] = jnp.zeros_like(total)

    def stats(j, carry):
        to = peer(j)
        kv_copy(0, to * 2 + other, kv_fwd.at[0, j], partner).wait_recv()
        mask = allowed(to)
        keys = pair_of(kk, to)
        for c in range(chunks):
            at = slice(c * lanes, (c + 1) * lanes)
            s = jnp.where(mask, dot(keys, q_cols[:, at]) * scale2, big_negative)
            if keep:
                scores[j, :, at] = s
            old = top[:, at]
            new = jnp.maximum(old, jnp.max(s, axis=0, keepdims=True))
            total[:, at] = total[:, at] * jnp.exp2(old - new) + jnp.sum(
                jnp.exp2(s - new), axis=0, keepdims=True
            )
            top[:, at] = new

        @pl.when(j + 1 < nz)
        def _():
            pass_on(1, j + 1, 0)

        return carry

    lax.fori_loop(0, nz, stats, 0)
    top[...] = top[...] + jnp.log(total[...]) * math.log2(math.e)
    dq_cols[...] = jnp.zeros_like(dq_cols)

    def to_partner(j):
        to = peer(j)
        return remote(
            part.at[to, other], from_partner.at[to], part_send.at[j], part_recv.at[j],
            "ctx", partner,
        )

    def to_owner(j):
        to = peer(j)
        return remote(
            z_out.at[j], z_in.at[j], z_send.at[j], z_recv.at[j], "ctx", to * 2 + side
        )

    def settle(j):
        to = peer(j)
        to_partner(j).wait_recv()
        both = part[to, side].astype(F32) + from_partner[to].astype(F32)
        z_out[j] = both.astype(BF16)
        to_owner(j).start()

    def grad(i, carry):
        j = lax.rem(i + 1, nz)
        to = peer(j)
        mask = None if keep else allowed(to)
        kv_copy(1, to * 2 + other, kv_fwd.at[1, j], partner).wait_recv()
        keys, values = pair_of(kk, to), pair_of(vv, to)
        for c in range(chunks):
            at = slice(c * lanes, (c + 1) * lanes)
            if keep:
                s = scores[j, :, at]
            else:
                s = jnp.where(mask, dot(keys, q_cols[:, at]) * scale2, big_negative)
            p = jnp.exp2(s - top[:, at])
            dp = dot(values, do_cols[:, at])
            p_b[:, at] = p.astype(BF16)
            ds_b[:, at] = (p * (dp - delta[:, at])).astype(BF16)
        dk = dot(ds_b[...], q_rows[...]) * scale
        dv = dot(p_b[...], do_rows[...])
        part[to, :, :, :head_dim] = dk.astype(BF16).reshape(2, tokens, head_dim)
        part[to, :, :, head_dim:] = dv.astype(BF16).reshape(2, tokens, head_dim)
        to_partner(j).start()
        dq_cols[...] += dot(keys.T, ds_b[...])

        @pl.when(i > 1)
        def _():
            settle(i - 1)

        return carry

    lax.fori_loop(0, nz, grad, 0)

    for h in range(heads):
        dq_b[h * head_dim:(h + 1) * head_dim, :] = (
            dq_cols[:, h * tokens:(h + 1) * tokens] * scale
        ).astype(BF16)
    tile = min(512, width)

    def query_terms(i, carry):
        at = pl.ds(pl.multiple_of(i * tile, tile), tile)
        grads[at, :] = dot(wq[at, :], dq_b[...])
        return carry

    early = max(1, width // tile // 4)
    lax.fori_loop(0, early, query_terms, 0)
    if nz > 1:
        settle(nz - 1)
    lax.fori_loop(early, width // tile, query_terms, 0)

    to_partner(0).wait_recv()
    mine = part[z, side].astype(F32) + from_partner[z].astype(F32)

    def gather_terms(j, acc):
        to_owner(j).wait_recv()
        return acc + z_in[j].astype(F32)

    mine = lax.fori_loop(1, nz, gather_terms, mine)
    dkv = mine.T.astype(BF16)

    size = features // pieces

    def rows_of(b, c, i):
        start = (lax.rem(pair + b, na) * 2 + c) * features + i * size
        return pl.ds(pl.multiple_of(start, size), size)

    def to_core(b, i):
        return remote(
            t_out.at[b, i], t_in.at[b, i], t_send.at[b, i], t_recv.at[b, i], "tp", t_partner
        )

    def across(b, i):
        to = lax.rem(pair + b, na) * 2 + core
        return remote(y_out.at[b, i], y_in.at[b, i], y_send.at[b, i], y_recv.at[b, i], "tp", to)

    for b in [b % na for b in range(1, na + 1)]:
        for i in range(pieces):
            at = rows_of(b, 1 - core, i)
            t_out[b, i] = (grads[at, :] + dot(wkv[at, :], dkv)).astype(BF16)
            to_core(b, i).start()
        for i in range(pieces):
            at = rows_of(b, core, i)
            term = grads[at, :] + dot(wkv[at, :], dkv)
            to_core(b, i).wait_recv()
            term = term + t_in[b, i].astype(F32)
            if b > 0:
                y_out[b, i] = term.astype(BF16)
                across(b, i).start()
            else:
                grads[at, :] = term
    for i in range(pieces):
        term = grads[rows_of(0, core, i), :]
        for b in range(1, na):
            across(b, i).wait_recv()
            term = term + y_in[b, i].astype(F32)
        out[:, i * size:(i + 1) * size] = term.T.astype(BF16)

    def drain(j, carry):
        forward(0, j).wait_send()
        forward(1, j).wait_send()
        to_partner(j).wait_send()
        return carry

    def drain_z(j, carry):
        kv_out(0, j).wait_send()
        kv_out(1, j).wait_send()
        to_owner(j).wait_send()
        return carry

    lax.fori_loop(0, nz, drain, 0)
    lax.fori_loop(1, nz, drain_z, 0)
    for b in range(na):
        for i in range(pieces):
            to_core(b, i).wait_send()
            if b > 0:
                across(b, i).wait_send()


def on_device(n, m, inputs, w_query, w_key, w_value, attn_out, d_out, block_order):
    tokens, width = inputs.shape
    head_dim = w_key.shape[1]
    local_width = w_query.shape[1]
    rows = local_width // head_dim * tokens
    features = width // m
    nz, na = n // 2, m // 2
    keep = n * tokens * rows * 4 <= kept_scores
    vmem, dma = pltpu.VMEM, pltpu.SemaphoreType.DMA
    block = (tokens, 2 * head_dim)
    scratch = [
        vmem((tokens, width), BF16),
        vmem((width, local_width), BF16),
        vmem((width, 2 * head_dim), BF16),
        vmem((tokens, local_width), BF16),
        vmem((tokens, local_width), BF16),
        vmem((tokens, local_width), F32),
        vmem((rows, head_dim), BF16),
        vmem((head_dim, rows), BF16),
        vmem((rows, head_dim), BF16),
        vmem((head_dim, rows), BF16),
        vmem((1, rows), F32),
        vmem((1, rows), F32),
        vmem((1, rows), F32),
        vmem((n, tokens, head_dim), BF16),
        vmem((n, tokens, head_dim), BF16),
        vmem((nz if keep else 1, 2 * tokens, rows), F32),
        vmem((2 * tokens, rows), BF16),
        vmem((2 * tokens, rows), BF16),
        vmem((head_dim, rows), F32),
        vmem((nz, 2, *block), BF16),
        vmem((nz, *block), BF16),
        vmem((nz, *block), BF16),
        vmem((nz, *block), BF16),
        vmem((local_width, tokens), BF16),
        vmem((width, tokens), F32),
        vmem((na, pieces, features // pieces, tokens), BF16),
        vmem((na, pieces, features // pieces, tokens), BF16),
        vmem((na, pieces, features // pieces, tokens), BF16),
        vmem((na, pieces, features // pieces, tokens), BF16),
        dma((4, q_chunks)), dma((2,)), dma((2, nz)), dma((2, nz)), dma((2, n)),
        dma((nz,)), dma((nz,)), dma((nz,)), dma((nz,)),
        dma((na, pieces)), dma((na, pieces)), dma((na, pieces)), dma((na, pieces)),
    ]
    seq = tokens * n
    flops = 2 * tokens * (2 * width * (local_width + 2 * head_dim) + 6 * seq * local_width)
    return pl.pallas_call(
        functools.partial(kernel, n, m),
        out_shape=pltpu.VMEM((tokens, features), BF16),
        in_specs=[pl.BlockSpec(memory_space=pltpu.SMEM)] + [pl.BlockSpec(memory_space=pl.ANY)] * 6,
        out_specs=pl.BlockSpec(memory_space=pltpu.VMEM),
        scratch_shapes=scratch,
        compiler_params=pltpu.CompilerParams(
            collective_id=0, has_side_effects=True, vmem_limit_bytes=58 * 2**20
        ),
        cost_estimate=pl.CostEstimate(
            flops=flops, bytes_accessed=2 * width * (local_width + 2 * head_dim + 2 * tokens),
            transcendentals=2 * rows * seq,
        ),
    )(block_order, inputs, w_query, w_key, w_value, attn_out, d_out)


def solution(mesh):
    placed = (
        P("ctx", None),
        P(None, "tp"),
        P(None, "tp"),
        P(None, "tp"),
        P("ctx", "tp"),
        P("ctx", "tp"),
        P(),
    )
    return jax.shard_map(
        functools.partial(on_device, mesh.shape["ctx"], mesh.shape["tp"]),
        mesh=mesh, in_specs=placed, out_specs=P("ctx", "tp"), check_vma=False,
    )
```

```python
import functools
import math

import jax
import jax.numpy as jnp
from jax import lax
from jax.experimental import pallas as pl
from jax.experimental.pallas import tpu as pltpu
from jax.sharding import PartitionSpec as P

MESH = pl.DeviceIdType.MESH
F32 = jnp.float32
BF16 = jnp.bfloat16
big_negative = -1e30
q_chunks = 4
pieces = 2
kept_scores = 8 * 2**20


def dot(a, b):
    return jnp.dot(a, b, preferred_element_type=F32)


def kernel(
    n, m, order, x_hbm, wq_hbm, wk_hbm, wv_hbm, ao_hbm, do_hbm, out,
    x, wq, wkv, ao, do, q_acc, q_rows, q_cols, do_rows, do_cols, delta, top, total,
    kk, vv, scores, p_b, ds_b, dq_cols, part, from_partner, z_out, z_in, dq_b, grads,
    t_out, t_in, y_out, y_in, own,
    load_sem, side_sem, kv_send, kv_fwd, kv_recv, part_send, part_recv, z_send, z_recv,
    t_send, t_recv, y_send, y_recv,
):
    tokens, width = x.shape
    head_dim = wk_hbm.shape[1]
    heads = wq.shape[1] // head_dim
    rows = heads * tokens
    span = tokens // 2
    scale = head_dim ** (-0.5)
    scale2 = scale * math.log2(math.e)
    nz, na = n // 2, m // 2
    me, mt = lax.axis_index("ctx"), lax.axis_index("tp")
    z, side = me // 2, lax.rem(me, 2)
    other = 1 - side
    partner = z * 2 + other
    pair, core = mt // 2, lax.rem(mt, 2)
    t_partner = pair * 2 + 1 - core
    features = width // m

    def peer(j):
        return lax.rem(z + j, nz)

    def local(src, dst, sem):
        return pltpu.make_async_copy(src, dst, sem)

    def remote(src, dst, send, recv, axis, to):
        return pltpu.make_async_remote_copy(
            src_ref=src, dst_ref=dst, send_sem=send, recv_sem=recv,
            device_id={axis: to}, device_id_type=MESH,
        )

    depth = width // q_chunks

    steps = [slice(i * depth, (i + 1) * depth) for i in range(q_chunks)]
    down = [pl.ds(i * depth, depth) for i in range(q_chunks)]
    x_loads = [
        local(x_hbm.at[:, d], x.at[:, d], load_sem.at[0, i]) for i, d in enumerate(down)
    ]
    wk_loads = [
        local(wk_hbm.at[d], wkv.at[d, pl.ds(0, head_dim)], load_sem.at[1, i])
        for i, d in enumerate(down)
    ]
    wv_loads = [
        local(wv_hbm.at[d], wkv.at[d, pl.ds(head_dim, head_dim)], load_sem.at[2, i])
        for i, d in enumerate(down)
    ]
    wq_loads = [local(wq_hbm.at[d], wq.at[d], load_sem.at[3, i]) for i, d in enumerate(down)]
    side_loads = [local(do_hbm, do, side_sem.at[0]), local(ao_hbm, ao, side_sem.at[1])]
    for i in range(q_chunks):
        x_loads[i].start()
        wk_loads[i].start()
    for copy in wv_loads + side_loads:
        copy.start()

    barrier = pltpu.get_barrier_semaphore()

    def greet(axis, to):
        pl.semaphore_signal(barrier, inc=1, device_id={axis: to}, device_id_type=MESH)

    greet("ctx", partner)
    greet("tp", t_partner)

    def greet_z(j, c):
        greet("ctx", peer(j) * 2 + side)
        return c

    lax.fori_loop(1, nz, greet_z, 0)
    for b in range(1, na):
        greet("tp", lax.rem(pair + b, na) * 2 + core)

    def kv_copy(kind, slot, send, to):
        held = (kk, vv)[kind]
        return remote(held.at[slot], held.at[slot], send, kv_recv.at[kind, slot], "ctx", to)

    def kv_out(kind, j):
        return kv_copy(kind, me, kv_send.at[kind, j], peer(j) * 2 + side)

    def forward(kind, j):
        return kv_copy(kind, peer(j) * 2 + side, kv_fwd.at[kind, j], partner)

    def send_own(kind):
        def start_out(j, c):
            kv_out(kind, j).start()
            return c

        lax.fori_loop(1, nz, start_out, 0)
        forward(kind, 0).start()

    def pass_on(kind, j, c):
        forward(kind, j).wait_recv()
        forward(kind, j).start()
        return c

    pass_key = functools.partial(pass_on, 0)

    keys = None
    for i in range(q_chunks):
        x_loads[i].wait()
        wk_loads[i].wait()
        wq_loads[i].start()
        piece = dot(x[:, steps[i]], wkv[steps[i], :head_dim])
        keys = piece if i == 0 else keys + piece
    kk[me] = keys.astype(BF16)
    pl.semaphore_wait(barrier, nz + na)
    send_own(0)
    for copy in wv_loads:
        copy.wait()
    vv[me] = dot(x[...], wkv[:, head_dim:]).astype(BF16)
    send_own(1)

    for copy in side_loads:
        copy.wait()
    for h in range(heads):
        r, c = slice(h * tokens, (h + 1) * tokens), slice(h * head_dim, (h + 1) * head_dim)
        do_h = do[:, c]
        do_rows[r, :] = do_h
        do_cols[:, r] = do_h.T
        both = do_h.astype(F32) * ao[:, c].astype(F32)
        delta[:, r] = jnp.sum(both.T, axis=0, keepdims=True)

    for i in range(q_chunks):
        wq_loads[i].wait()
        piece = dot(x[:, steps[i]], wq[steps[i], :])
        q_acc[...] = piece if i == 0 else q_acc[...] + piece
        last = nz if i == q_chunks - 2 else min(i + 2, nz)
        if i < q_chunks - 1:
            lax.fori_loop(min(i + 1, nz), last, pass_key, 0)
    for h in range(heads):
        r, c = slice(h * tokens, (h + 1) * tokens), slice(h * head_dim, (h + 1) * head_dim)
        q_h = q_acc[:, c].astype(BF16)
        q_rows[r, :] = q_h
        q_cols[:, r] = q_h.T

    lanes = max(2 * tokens, 256) if heads % 2 == 0 else tokens
    chunks = rows // lanes
    lane = lax.rem(lax.broadcasted_iota(jnp.int32, (1, lanes), 1), tokens)
    o0, o1 = order[me * 2], order[me * 2 + 1]
    query_pos = jnp.where(lane < span, o0 * span + lane, o1 * span + lane - span)
    key_row = lax.broadcasted_iota(jnp.int32, (2 * tokens, 1), 0)

    def allowed(to):
        key_pos = order[to * 4] * span + key_row
        for i in range(1, 4):
            key_pos = jnp.where(
                key_row >= i * span, order[to * 4 + i] * span + key_row - i * span, key_pos
            )
        return key_pos <= query_pos

    def pair_of(held, to):
        return held[pl.ds(to * 2, 2)].reshape(2 * tokens, head_dim)

    keep = scores.shape[0] == nz
    top[...] = jnp.full_like(top, big_negative)
    total[...] = jnp.zeros_like(total)

    def stats(j, carry):
        to = peer(j)
        kv_copy(0, to * 2 + other, kv_fwd.at[0, j], partner).wait_recv()
        mask = allowed(to)
        keys = pair_of(kk, to)
        for c in range(chunks):
            at = slice(c * lanes, (c + 1) * lanes)
            s = jnp.where(mask, dot(keys, q_cols[:, at]) * scale2, big_negative)
            if keep:
                scores[j, :, at] = s
            old = top[:, at]
            new = jnp.maximum(old, jnp.max(s, axis=0, keepdims=True))
            total[:, at] = total[:, at] * jnp.exp2(old - new) + jnp.sum(
                jnp.exp2(s - new), axis=0, keepdims=True
            )
            top[:, at] = new

        @pl.when(j + 1 < nz)
        def _():
            pass_on(1, j + 1, 0)

        return carry

    lax.fori_loop(0, nz, stats, 0)
    top[...] = top[...] + jnp.log(total[...]) * math.log2(math.e)
    dq_cols[...] = jnp.zeros_like(dq_cols)

    groups = nz // 2

    def pairs_of(g):
        return 2 * g + 1, lax.rem(2 * g + 2, nz)

    def to_partner(t):
        return remote(
            part.at[t, other], from_partner.at[t], part_send.at[t], part_recv.at[t],
            "ctx", partner,
        )

    def to_owner(u, j):
        t, a = u * groups + (j - 1) // 2, lax.rem(j - 1, 2)
        return remote(
            z_out.at[t, a], z_in.at[u, j], z_send.at[u, j], z_recv.at[u, j],
            "ctx", peer(j) * 2 + side,
        )

    def settle(t):
        u = t // groups
        j, j_next = pairs_of(lax.rem(t, groups))
        to_partner(t).wait_recv()
        both = part[t, side].astype(F32) + from_partner[t].astype(F32)
        z_out[t] = both.astype(BF16)
        to_owner(u, j).start()

        @pl.when(j_next != 0)
        def _():
            to_owner(u, j_next).start()

    half_lane = lax.rem(lax.broadcasted_iota(jnp.int32, (2 * tokens, 1), 0), span)

    def grad(t, carry):
        u, g = t // groups, lax.rem(t, groups)
        js = pairs_of(g)
        at_u = pl.ds(pl.multiple_of(u * span, span), span)

        @pl.when(u == 0)
        def _():
            for j in js:
                kv_copy(1, peer(j) * 2 + other, kv_fwd.at[1, j], partner).wait_recv()

        blocks = [(j, d) for d in range(2) for j in js]

        def rows_from(held):
            return jnp.concatenate([held[peer(j) * 2 + d, at_u] for j, d in blocks], axis=0)

        keys, values = rows_from(kk), rows_from(vv)
        if not keep:
            row = lax.broadcasted_iota(jnp.int32, (2 * tokens, 1), 0)
            key_pos = None
            for i, (j, d) in enumerate(blocks):
                pos = order[(peer(j) * 2 + d) * 2 + u] * span + half_lane
                key_pos = pos if i == 0 else jnp.where(row >= i * span, pos, key_pos)
            mask = key_pos <= query_pos
        for c in range(chunks):
            at = slice(c * lanes, (c + 1) * lanes)
            if keep:
                s = jnp.concatenate([
                    scores[j, pl.ds(pl.multiple_of(d * tokens + u * span, span), span), at]
                    for j, d in blocks
                ], axis=0)
            else:
                s = jnp.where(mask, dot(keys, q_cols[:, at]) * scale2, big_negative)
            p = jnp.exp2(s - top[:, at])
            dp = dot(values, do_cols[:, at])
            p_b[:, at] = p.astype(BF16)
            ds_b[:, at] = (p * (dp - delta[:, at])).astype(BF16)
        dk = dot(ds_b[...], q_rows[...]) * scale
        dv = dot(p_b[...], do_rows[...])
        part[t, :, :, :, :head_dim] = dk.astype(BF16).reshape(2, 2, span, head_dim)
        part[t, :, :, :, head_dim:] = dv.astype(BF16).reshape(2, 2, span, head_dim)
        to_partner(t).start()
        dq_cols[...] += dot(keys.T, ds_b[...])

        @pl.when(t > 1)
        def _():
            settle(t - 2)

        return carry

    lax.fori_loop(0, nz, grad, 0)

    for h in range(heads):
        dq_b[h * head_dim:(h + 1) * head_dim, :] = (
            dq_cols[:, h * tokens:(h + 1) * tokens] * scale
        ).astype(BF16)
    low = lax.broadcasted_iota(jnp.int32, (1, 1, tokens), 2) < span
    tile = 4 * tokens

    def query_terms(i, carry):
        at = pl.ds(pl.multiple_of(i * tile, tile), tile)
        to = pl.ds(pl.multiple_of(i * (tile // 2), tile // 2), tile // 2)
        terms = dot(wq[at, :], dq_b[...])
        turned = pltpu.roll(terms, span, 1).reshape(2, 2, tokens, tokens)
        terms = terms.reshape(2, 2, tokens, tokens)
        grads[0, to, :] = jnp.where(low, terms[:, 0], turned[:, 1]).reshape(tile // 2, tokens)
        grads[1, to, :] = jnp.where(low, turned[:, 0], terms[:, 1]).reshape(tile // 2, tokens)
        return carry

    tiles = width // tile
    early = max(1, tiles * 5 // 8)
    lax.fori_loop(0, early, query_terms, 0)
    settle(nz - 2)
    lax.fori_loop(early, tiles, query_terms, 0)
    settle(nz - 1)

    size = features // 2 // pieces

    def rows_of(b, c, i):
        return (lax.rem(pair + b, na) * 2 + c) * (features // 2) + i * size

    def to_core(u, b, i):
        return remote(
            t_out.at[u, b, i], t_in.at[u, b, i], t_send.at[u, b, i], t_recv.at[u, b, i],
            "tp", t_partner,
        )

    def across(u, b, i):
        to = lax.rem(pair + b, na) * 2 + core
        return remote(
            y_out.at[u, b, i], y_in.at[u, b, i], y_send.at[u, b, i], y_recv.at[u, b, i], "tp", to
        )

    for u in range(2):
        def gather_terms(j, acc):
            to_owner(u, j).wait_recv()
            return acc + z_in[u, j].astype(F32)

        mine = z_out[u * groups + groups - 1, 1].astype(F32)
        mine = lax.fori_loop(1, nz, gather_terms, mine)
        dkv = jnp.concatenate([mine, mine], axis=0).T.astype(BF16)

        def term_of(b, c, i):
            start = rows_of(b, c, i)
            wide = pl.ds(pl.multiple_of(start * 2, size * 2), size * 2)
            terms = dot(wkv[wide, :], dkv).reshape(size // tokens, 2, tokens, tokens)
            terms = jnp.where(low, terms[:, 0], terms[:, 1]).reshape(size, tokens)
            return grads[u, pl.ds(pl.multiple_of(start, size), size), :] + terms

        for b in [b % na for b in range(1, na + 1)]:
            for i in range(pieces):
                t_out[u, b, i] = term_of(b, 1 - core, i).astype(BF16)
                to_core(u, b, i).start()
            for i in range(pieces):
                term = term_of(b, core, i)
                to_core(u, b, i).wait_recv()
                term = term + t_in[u, b, i].astype(F32)
                if b > 0:
                    y_out[u, b, i] = term.astype(BF16)
                    across(u, b, i).start()
                else:
                    own[u, i] = term
    for u in range(2):
        for i in range(pieces):
            term = own[u, i]
            for b in range(1, na):
                across(u, b, i).wait_recv()
                term = term + y_in[u, b, i].astype(F32)
            for k in range(size // tokens):
                block = term[k * tokens:(k + 1) * tokens].T.astype(BF16)
                for d in range(2):
                    at = (i * size + k * tokens) * 2 + d * tokens
                    out[u * span:(u + 1) * span, at:at + tokens] = block[d * span:(d + 1) * span]

    def drain(j, carry):
        forward(0, j).wait_send()
        forward(1, j).wait_send()
        to_partner(j).wait_send()
        return carry

    def drain_z(j, carry):
        kv_out(0, j).wait_send()
        kv_out(1, j).wait_send()
        to_owner(0, j).wait_send()
        to_owner(1, j).wait_send()
        return carry

    lax.fori_loop(0, nz, drain, 0)
    lax.fori_loop(1, nz, drain_z, 0)
    for u in range(2):
        for b in range(na):
            for i in range(pieces):
                to_core(u, b, i).wait_send()
                if b > 0:
                    across(u, b, i).wait_send()


def on_device(n, m, inputs, w_query, w_key, w_value, attn_out, d_out, block_order):
    tokens, width = inputs.shape
    head_dim = w_key.shape[1]
    local_width = w_query.shape[1]
    rows = local_width // head_dim * tokens
    features = width // m
    nz, na = n // 2, m // 2
    keep = n * tokens * rows * 4 <= kept_scores
    vmem, dma = pltpu.VMEM, pltpu.SemaphoreType.DMA
    half = (tokens // 2, 2 * head_dim)
    piece = (pieces, features // 2 // pieces, tokens)
    scratch = [
        vmem((tokens, width), BF16),
        vmem((width, local_width), BF16),
        vmem((width, 2 * head_dim), BF16),
        vmem((tokens, local_width), BF16),
        vmem((tokens, local_width), BF16),
        vmem((tokens, local_width), F32),
        vmem((rows, head_dim), BF16),
        vmem((head_dim, rows), BF16),
        vmem((rows, head_dim), BF16),
        vmem((head_dim, rows), BF16),
        vmem((1, rows), F32),
        vmem((1, rows), F32),
        vmem((1, rows), F32),
        vmem((n, tokens, head_dim), BF16),
        vmem((n, tokens, head_dim), BF16),
        vmem((nz if keep else 1, 2 * tokens, rows), F32),
        vmem((2 * tokens, rows), BF16),
        vmem((2 * tokens, rows), BF16),
        vmem((head_dim, rows), F32),
        vmem((nz, 2, 2, *half), BF16),
        vmem((nz, 2, *half), BF16),
        vmem((nz, 2, *half), BF16),
        vmem((2, nz, *half), BF16),
        vmem((local_width, tokens), BF16),
        vmem((2, width // 2, tokens), F32),
        vmem((2, na, *piece), BF16),
        vmem((2, na, *piece), BF16),
        vmem((2, na, *piece), BF16),
        vmem((2, na, *piece), BF16),
        vmem((2, *piece), F32),
        dma((4, q_chunks)), dma((2,)), dma((2, nz)), dma((2, nz)), dma((2, n)),
        dma((nz,)), dma((nz,)), dma((2, nz)), dma((2, nz)),
        *[dma((2, na, pieces)) for _ in range(4)],
    ]
    seq = tokens * n
    flops = 2 * tokens * (2 * width * (local_width + 2 * head_dim) + 6 * seq * local_width)
    return pl.pallas_call(
        functools.partial(kernel, n, m),
        out_shape=pltpu.VMEM((tokens, features), BF16),
        in_specs=[pl.BlockSpec(memory_space=pltpu.SMEM)] + [pl.BlockSpec(memory_space=pl.ANY)] * 6,
        out_specs=pl.BlockSpec(memory_space=pltpu.VMEM),
        scratch_shapes=scratch,
        compiler_params=pltpu.CompilerParams(
            collective_id=0, has_side_effects=True, vmem_limit_bytes=58 * 2**20
        ),
        cost_estimate=pl.CostEstimate(
            flops=flops, bytes_accessed=2 * width * (local_width + 2 * head_dim + 2 * tokens),
            transcendentals=2 * rows * seq,
        ),
    )(block_order, inputs, w_query, w_key, w_value, attn_out, d_out)


def solution(mesh):
    placed = (
        P("ctx", None),
        P(None, "tp"),
        P(None, "tp"),
        P(None, "tp"),
        P("ctx", "tp"),
        P("ctx", "tp"),
        P(),
    )
    return jax.shard_map(
        functools.partial(on_device, mesh.shape["ctx"], mesh.shape["tp"]),
        mesh=mesh, in_specs=placed, out_specs=P("ctx", "tp"), check_vma=False,
    )
```

```python
import functools
import math

import jax
import jax.numpy as jnp
from jax import lax
from jax.experimental import pallas as pl
from jax.experimental.pallas import tpu as pltpu
from jax.sharding import PartitionSpec as P

MESH = pl.DeviceIdType.MESH
F32 = jnp.float32
BF16 = jnp.bfloat16
big_negative = -1e30
q_chunks = 4
pieces = 4
kept_scores = 8 * 2**20


def dot(a, b):
    return jnp.dot(a, b, preferred_element_type=F32)


def kernel(
    n, m, order, x_hbm, wq_hbm, wk_hbm, wv_hbm, ao_hbm, do_hbm, out,
    x, wq, wkv, ao, do, q_acc, q_rows, q_cols, do_rows, do_cols, delta, top, total,
    kv, scores, p_b, ds_b, dq_cols, part, from_partner, z_out, z_in, dq_b, grads,
    t_out, t_in, y_out, y_in,
    load_sem, side_sem, kv_send, kv_fwd, kv_recv, part_send, part_recv, z_send, z_recv,
    t_send, t_recv, y_send, y_recv,
):
    tokens, width = x.shape
    head_dim = wk_hbm.shape[1]
    heads = wq.shape[1] // head_dim
    rows = heads * tokens
    span = tokens // 2
    scale = head_dim ** (-0.5)
    scale2 = scale * math.log2(math.e)
    nz, na = n // 2, m // 2
    me, mt = lax.axis_index("ctx"), lax.axis_index("tp")
    z, side = me // 2, lax.rem(me, 2)
    other = 1 - side
    partner = z * 2 + other
    pair, core = mt // 2, lax.rem(mt, 2)
    t_partner = pair * 2 + 1 - core
    features = width // m

    def peer(j):
        return lax.rem(z + j, nz)

    def local(src, dst, sem):
        return pltpu.make_async_copy(src, dst, sem)

    def remote(src, dst, send, recv, axis, to):
        return pltpu.make_async_remote_copy(
            src_ref=src, dst_ref=dst, send_sem=send, recv_sem=recv,
            device_id={axis: to}, device_id_type=MESH,
        )

    depth = width // q_chunks

    steps = [slice(i * depth, (i + 1) * depth) for i in range(q_chunks)]
    down = [pl.ds(i * depth, depth) for i in range(q_chunks)]
    x_loads = [
        local(x_hbm.at[:, d], x.at[:, d], load_sem.at[0, i]) for i, d in enumerate(down)
    ]
    wk_loads = [
        local(wk_hbm.at[d], wkv.at[d, pl.ds(0, head_dim)], load_sem.at[1, i])
        for i, d in enumerate(down)
    ]
    wv_loads = [
        local(wv_hbm.at[d], wkv.at[d, pl.ds(head_dim, head_dim)], load_sem.at[2, i])
        for i, d in enumerate(down)
    ]
    wq_loads = [local(wq_hbm.at[d], wq.at[d], load_sem.at[3, i]) for i, d in enumerate(down)]
    side_loads = [local(do_hbm, do, side_sem.at[0]), local(ao_hbm, ao, side_sem.at[1])]
    for i in range(q_chunks):
        x_loads[i].start()
        wk_loads[i].start()
        wv_loads[i].start()
    for copy in side_loads:
        copy.start()

    barrier = pltpu.get_barrier_semaphore()

    def greet(axis, to):
        pl.semaphore_signal(barrier, inc=1, device_id={axis: to}, device_id_type=MESH)

    greet("ctx", partner)
    greet("tp", t_partner)

    def greet_z(j, c):
        greet("ctx", peer(j) * 2 + side)
        return c

    lax.fori_loop(1, nz, greet_z, 0)
    for b in range(1, na):
        greet("tp", lax.rem(pair + b, na) * 2 + core)

    def kv_copy(slot, send, to):
        return remote(kv.at[slot], kv.at[slot], send, kv_recv.at[slot], "ctx", to)

    def kv_out(j):
        return kv_copy(me, kv_send.at[j], peer(j) * 2 + side)

    def forward(j):
        return kv_copy(peer(j) * 2 + side, kv_fwd.at[j], partner)

    def start_out(j, c):
        kv_out(j).start()
        return c

    def pass_on(j, c):
        forward(j).wait_recv()
        forward(j).start()
        return c

    mine = None
    for i in range(q_chunks):
        x_loads[i].wait()
        wk_loads[i].wait()
        wv_loads[i].wait()
        wq_loads[i].start()
        piece = dot(x[:, steps[i]], wkv[steps[i], :])
        mine = piece if i == 0 else mine + piece
    kv[me] = mine.astype(BF16)
    pl.semaphore_wait(barrier, nz + na)
    lax.fori_loop(1, nz, start_out, 0)
    forward(0).start()

    for copy in side_loads:
        copy.wait()
    for h in range(heads):
        r, c = slice(h * tokens, (h + 1) * tokens), slice(h * head_dim, (h + 1) * head_dim)
        do_h = do[:, c]
        do_rows[r, :] = do_h
        do_cols[:, r] = do_h.T
        both = do_h.astype(F32) * ao[:, c].astype(F32)
        delta[:, r] = jnp.sum(both.T, axis=0, keepdims=True)

    for i in range(q_chunks):
        wq_loads[i].wait()
        piece = dot(x[:, steps[i]], wq[steps[i], :])
        q_acc[...] = piece if i == 0 else q_acc[...] + piece
        last = nz if i == q_chunks - 2 else min(i + 2, nz)
        if i < q_chunks - 1:
            lax.fori_loop(min(i + 1, nz), last, pass_on, 0)
    for h in range(heads):
        r, c = slice(h * tokens, (h + 1) * tokens), slice(h * head_dim, (h + 1) * head_dim)
        q_h = q_acc[:, c].astype(BF16)
        q_rows[r, :] = q_h
        q_cols[:, r] = q_h.T

    lanes = max(2 * tokens, 256) if heads % 2 == 0 else tokens
    chunks = rows // lanes
    lane = lax.rem(lax.broadcasted_iota(jnp.int32, (1, lanes), 1), tokens)
    o0, o1 = order[me * 2], order[me * 2 + 1]
    query_pos = jnp.where(lane < span, o0 * span + lane, o1 * span + lane - span)
    span_row = lax.broadcasted_iota(jnp.int32, (span, 1), 0)

    def allowed(slots):
        key_pos = [order[slot * 2 + i] * span + span_row for slot in slots for i in range(2)]
        return jnp.concatenate(key_pos, axis=0) <= query_pos

    def arrived(j, carry):
        kv_copy(peer(j) * 2 + other, kv_fwd.at[j], partner).wait_recv()
        return carry

    lax.fori_loop(0, nz, arrived, 0)
    keep = scores.shape[0] == n * tokens
    top[...] = jnp.full_like(top, big_negative)
    total[...] = jnp.zeros_like(total)
    wide = min(n, 8)

    def stats(i, carry):
        mask = allowed([i * wide + d for d in range(wide)])
        keys = kv[pl.ds(i * wide, wide)].reshape(wide * tokens, 2 * head_dim)[:, :head_dim]
        for c in range(chunks):
            at = slice(c * lanes, (c + 1) * lanes)
            s = jnp.where(mask, dot(keys, q_cols[:, at]) * scale2, big_negative)
            if keep:
                scores[:, at] = s
            old = top[:, at]
            new = jnp.maximum(old, jnp.max(s, axis=0, keepdims=True))
            total[:, at] = total[:, at] * jnp.exp2(old - new) + jnp.sum(
                jnp.exp2(s - new), axis=0, keepdims=True
            )
            top[:, at] = new
        return carry

    if n == wide:
        stats(0, 0)
    else:
        lax.fori_loop(0, n // wide, stats, 0)
    top[...] = top[...] + jnp.log(total[...]) * math.log2(math.e)
    dq_cols[...] = jnp.zeros_like(dq_cols)

    def to_partner(j):
        to = peer(j)
        return remote(
            part.at[to, other], from_partner.at[to], part_send.at[j], part_recv.at[j],
            "ctx", partner,
        )

    def to_owner(j):
        to = peer(j)
        return remote(
            z_out.at[j], z_in.at[j], z_send.at[j], z_recv.at[j], "ctx", to * 2 + side
        )

    def settle(j):
        to = peer(j)
        to_partner(j).wait_recv()
        both = part[to, side].astype(F32) + from_partner[to].astype(F32)
        z_out[j] = both.astype(BF16)
        to_owner(j).start()

    def grad(i, carry):
        js = (2 * i + 1, lax.rem(2 * i + 2, nz))
        mask = None if keep else allowed([peer(j) * 2 + d for j in js for d in range(2)])

        def pair_rows(j):
            return pl.ds(pl.multiple_of(peer(j) * 2 * tokens, 2 * tokens), 2 * tokens)

        both = jnp.concatenate(
            [kv[pl.ds(peer(j) * 2, 2)].reshape(2 * tokens, 2 * head_dim) for j in js], axis=0
        )
        keys, values = both[:, :head_dim], both[:, head_dim:]
        for c in range(chunks):
            at = slice(c * lanes, (c + 1) * lanes)
            if keep:
                s = jnp.concatenate([scores[pair_rows(j), at] for j in js], axis=0)
            else:
                s = jnp.where(mask, dot(keys, q_cols[:, at]) * scale2, big_negative)
            p = jnp.exp2(s - top[:, at])
            dp = dot(values, do_cols[:, at])
            p_b[:, at] = p.astype(BF16)
            ds_b[:, at] = (p * (dp - delta[:, at])).astype(BF16)
        dk = (dot(ds_b[...], q_rows[...]) * scale).astype(BF16)
        dv = dot(p_b[...], do_rows[...]).astype(BF16)
        for a, j in enumerate(js):
            r = slice(a * 2 * tokens, (a + 1) * 2 * tokens)
            part[peer(j), :, :, :head_dim] = dk[r].reshape(2, tokens, head_dim)
            part[peer(j), :, :, head_dim:] = dv[r].reshape(2, tokens, head_dim)
            to_partner(j).start()
        dq_cols[...] += dot(keys.T, ds_b[...])

        @pl.when(i > 0)
        def _():
            settle(2 * i - 1)
            settle(2 * i)

        return carry

    lax.fori_loop(0, nz // 2, grad, 0)

    for h in range(heads):
        dq_b[h * head_dim:(h + 1) * head_dim, :] = (
            dq_cols[:, h * tokens:(h + 1) * tokens] * scale
        ).astype(BF16)
    tile = min(1024, width)

    def query_terms(i, carry):
        at = pl.ds(pl.multiple_of(i * tile, tile), tile)
        grads[at, :] = dot(wq[at, :], dq_b[...])
        return carry

    early = max(1, width // tile // 4)
    lax.fori_loop(0, early, query_terms, 0)
    settle(nz - 1)
    lax.fori_loop(early, width // tile, query_terms, 0)

    to_partner(0).wait_recv()
    mine = part[z, side].astype(F32) + from_partner[z].astype(F32)

    def gather_terms(j, acc):
        to_owner(j).wait_recv()
        return acc + z_in[j].astype(F32)

    mine = lax.fori_loop(1, nz, gather_terms, mine)
    dkv = mine.T.astype(BF16)

    size = features // pieces

    def rows_of(b, c, i):
        start = (lax.rem(pair + b, na) * 2 + c) * features + i * size
        return pl.ds(pl.multiple_of(start, size), size)

    def to_core(b, i):
        return remote(
            t_out.at[b, i], t_in.at[b, i], t_send.at[b, i], t_recv.at[b, i], "tp", t_partner
        )

    def across(b, i):
        to = lax.rem(pair + b, na) * 2 + core
        return remote(y_out.at[b, i], y_in.at[b, i], y_send.at[b, i], y_recv.at[b, i], "tp", to)

    for b in [b % na for b in range(1, na + 1)]:
        for i in range(pieces):
            at = rows_of(b, 1 - core, i)
            t_out[b, i] = (grads[at, :] + dot(wkv[at, :], dkv)).astype(BF16)
            to_core(b, i).start()
        for i in range(pieces):
            at = rows_of(b, core, i)
            term = grads[at, :] + dot(wkv[at, :], dkv)
            to_core(b, i).wait_recv()
            term = term + t_in[b, i].astype(F32)
            if b > 0:
                y_out[b, i] = term.astype(BF16)
                across(b, i).start()
            else:
                grads[at, :] = term
    for i in range(pieces):
        term = grads[rows_of(0, core, i), :]
        for b in range(1, na):
            across(b, i).wait_recv()
            term = term + y_in[b, i].astype(F32)
        out[:, i * size:(i + 1) * size] = term.T.astype(BF16)

    def drain(j, carry):
        forward(j).wait_send()
        to_partner(j).wait_send()
        return carry

    def drain_z(j, carry):
        kv_out(j).wait_send()
        to_owner(j).wait_send()
        return carry

    lax.fori_loop(0, nz, drain, 0)
    lax.fori_loop(1, nz, drain_z, 0)
    for b in range(na):
        for i in range(pieces):
            to_core(b, i).wait_send()
            if b > 0:
                across(b, i).wait_send()


def on_device(n, m, inputs, w_query, w_key, w_value, attn_out, d_out, block_order):
    tokens, width = inputs.shape
    head_dim = w_key.shape[1]
    local_width = w_query.shape[1]
    rows = local_width // head_dim * tokens
    features = width // m
    nz, na = n // 2, m // 2
    keep = n * tokens * rows * 4 <= kept_scores
    vmem, dma = pltpu.VMEM, pltpu.SemaphoreType.DMA
    block = (tokens, 2 * head_dim)
    scratch = [
        vmem((tokens, width), BF16),
        vmem((width, local_width), BF16),
        vmem((width, 2 * head_dim), BF16),
        vmem((tokens, local_width), BF16),
        vmem((tokens, local_width), BF16),
        vmem((tokens, local_width), F32),
        vmem((rows, head_dim), BF16),
        vmem((head_dim, rows), BF16),
        vmem((rows, head_dim), BF16),
        vmem((head_dim, rows), BF16),
        vmem((1, rows), F32),
        vmem((1, rows), F32),
        vmem((1, rows), F32),
        vmem((n, *block), BF16),
        vmem((n * tokens if keep else 8, rows), F32),
        vmem((4 * tokens, rows), BF16),
        vmem((4 * tokens, rows), BF16),
        vmem((head_dim, rows), F32),
        vmem((nz, 2, *block), BF16),
        vmem((nz, *block), BF16),
        vmem((nz, *block), BF16),
        vmem((nz, *block), BF16),
        vmem((local_width, tokens), BF16),
        vmem((width, tokens), F32),
        vmem((na, pieces, features // pieces, tokens), BF16),
        vmem((na, pieces, features // pieces, tokens), BF16),
        vmem((na, pieces, features // pieces, tokens), BF16),
        vmem((na, pieces, features // pieces, tokens), BF16),
        dma((4, q_chunks)), dma((2,)), dma((nz,)), dma((nz,)), dma((n,)),
        dma((nz,)), dma((nz,)), dma((nz,)), dma((nz,)),
        dma((na, pieces)), dma((na, pieces)), dma((na, pieces)), dma((na, pieces)),
    ]
    seq = tokens * n
    flops = 2 * tokens * (2 * width * (local_width + 2 * head_dim) + 6 * seq * local_width)
    return pl.pallas_call(
        functools.partial(kernel, n, m),
        out_shape=pltpu.VMEM((tokens, features), BF16),
        in_specs=[pl.BlockSpec(memory_space=pltpu.SMEM)] + [pl.BlockSpec(memory_space=pl.ANY)] * 6,
        out_specs=pl.BlockSpec(memory_space=pltpu.VMEM),
        scratch_shapes=scratch,
        compiler_params=pltpu.CompilerParams(
            collective_id=0, has_side_effects=True, vmem_limit_bytes=58 * 2**20
        ),
        cost_estimate=pl.CostEstimate(
            flops=flops, bytes_accessed=2 * width * (local_width + 2 * head_dim + 2 * tokens),
            transcendentals=2 * rows * seq,
        ),
    )(block_order, inputs, w_query, w_key, w_value, attn_out, d_out)


def solution(mesh):
    placed = (
        P("ctx", None),
        P(None, "tp"),
        P(None, "tp"),
        P(None, "tp"),
        P("ctx", "tp"),
        P("ctx", "tp"),
        P(),
    )
    return jax.shard_map(
        functools.partial(on_device, mesh.shape["ctx"], mesh.shape["tp"]),
        mesh=mesh, in_specs=placed, out_specs=P("ctx", "tp"), check_vma=False,
    )
```

```python
import functools
import math

import jax
import jax.numpy as jnp
from jax import lax
from jax.experimental import pallas as pl
from jax.experimental.pallas import tpu as pltpu
from jax.sharding import PartitionSpec as P

MESH = pl.DeviceIdType.MESH
F32 = jnp.float32
BF16 = jnp.bfloat16
big_negative = -1e30
q_chunks = 4
pieces = 4
kept_scores = 8 * 2**20


def dot(a, b):
    return jnp.dot(a, b, preferred_element_type=F32)


def kernel(
    n, m, order, x_hbm, wq_hbm, wk_hbm, wv_hbm, ao_hbm, do_hbm, out,
    x, wq, wkv, ao, do, q_acc, q_rows, q_cols, do_rows, do_cols, delta, top, total,
    kk, vv, scores, p_b, ds_b, dq_cols, part, from_partner, z_out, z_in, dq_b, grads,
    t_out, t_in, y_out, y_in,
    load_sem, side_sem, kv_send, kv_fwd, kv_recv, part_send, part_recv, z_send, z_recv,
    t_send, t_recv, y_send, y_recv,
):
    tokens, width = x.shape
    head_dim = wk_hbm.shape[1]
    heads = wq.shape[1] // head_dim
    rows = heads * tokens
    span = tokens // 2
    scale = head_dim ** (-0.5)
    scale2 = scale * math.log2(math.e)
    nz, na = n // 2, m // 2
    me, mt = lax.axis_index("ctx"), lax.axis_index("tp")
    z, side = me // 2, lax.rem(me, 2)
    other = 1 - side
    partner = z * 2 + other
    pair, core = mt // 2, lax.rem(mt, 2)
    t_partner = pair * 2 + 1 - core
    features = width // m

    def peer(j):
        return lax.rem(z + j, nz)

    def local(src, dst, sem):
        return pltpu.make_async_copy(src, dst, sem)

    def remote(src, dst, send, recv, axis, to):
        return pltpu.make_async_remote_copy(
            src_ref=src, dst_ref=dst, send_sem=send, recv_sem=recv,
            device_id={axis: to}, device_id_type=MESH,
        )

    depth = width // q_chunks

    steps = [slice(i * depth, (i + 1) * depth) for i in range(q_chunks)]
    down = [pl.ds(i * depth, depth) for i in range(q_chunks)]
    x_loads = [
        local(x_hbm.at[:, d], x.at[:, d], load_sem.at[0, i]) for i, d in enumerate(down)
    ]
    wk_loads = [
        local(wk_hbm.at[d], wkv.at[d, pl.ds(0, head_dim)], load_sem.at[1, i])
        for i, d in enumerate(down)
    ]
    wv_loads = [
        local(wv_hbm.at[d], wkv.at[d, pl.ds(head_dim, head_dim)], load_sem.at[2, i])
        for i, d in enumerate(down)
    ]
    wq_loads = [local(wq_hbm.at[d], wq.at[d], load_sem.at[3, i]) for i, d in enumerate(down)]
    side_loads = [local(do_hbm, do, side_sem.at[0]), local(ao_hbm, ao, side_sem.at[1])]
    for i in range(q_chunks):
        x_loads[i].start()
        wk_loads[i].start()
    for copy in wv_loads + side_loads:
        copy.start()

    barrier = pltpu.get_barrier_semaphore()

    def greet(axis, to):
        pl.semaphore_signal(barrier, inc=1, device_id={axis: to}, device_id_type=MESH)

    greet("ctx", partner)
    greet("tp", t_partner)

    def greet_z(j, c):
        greet("ctx", peer(j) * 2 + side)
        return c

    lax.fori_loop(1, nz, greet_z, 0)
    for b in range(1, na):
        greet("tp", lax.rem(pair + b, na) * 2 + core)

    def kv_copy(kind, slot, send, to):
        held = (kk, vv)[kind]
        return remote(held.at[slot], held.at[slot], send, kv_recv.at[kind, slot], "ctx", to)

    def kv_out(kind, j):
        return kv_copy(kind, me, kv_send.at[kind, j], peer(j) * 2 + side)

    def forward(kind, j):
        return kv_copy(kind, peer(j) * 2 + side, kv_fwd.at[kind, j], partner)

    def send_own(kind):
        def start_out(j, c):
            kv_out(kind, j).start()
            return c

        lax.fori_loop(1, nz, start_out, 0)
        forward(kind, 0).start()

    def pass_on(kind, j, c):
        forward(kind, j).wait_recv()
        forward(kind, j).start()
        return c

    pass_key = functools.partial(pass_on, 0)

    keys = None
    for i in range(q_chunks):
        x_loads[i].wait()
        wk_loads[i].wait()
        wq_loads[i].start()
        piece = dot(x[:, steps[i]], wkv[steps[i], :head_dim])
        keys = piece if i == 0 else keys + piece
    kk[me] = keys.astype(BF16)
    pl.semaphore_wait(barrier, nz + na)
    send_own(0)
    for copy in wv_loads:
        copy.wait()
    vv[me] = dot(x[...], wkv[:, head_dim:]).astype(BF16)
    send_own(1)

    for copy in side_loads:
        copy.wait()
    for h in range(heads):
        r, c = slice(h * tokens, (h + 1) * tokens), slice(h * head_dim, (h + 1) * head_dim)
        do_h = do[:, c]
        do_rows[r, :] = do_h
        do_cols[:, r] = do_h.T
        both = do_h.astype(F32) * ao[:, c].astype(F32)
        delta[:, r] = jnp.sum(both.T, axis=0, keepdims=True)

    for i in range(q_chunks):
        wq_loads[i].wait()
        piece = dot(x[:, steps[i]], wq[steps[i], :])
        q_acc[...] = piece if i == 0 else q_acc[...] + piece
        last = nz if i == q_chunks - 2 else min(i + 2, nz)
        if i < q_chunks - 1:
            lax.fori_loop(min(i + 1, nz), last, pass_key, 0)
    for h in range(heads):
        r, c = slice(h * tokens, (h + 1) * tokens), slice(h * head_dim, (h + 1) * head_dim)
        q_h = q_acc[:, c].astype(BF16)
        q_rows[r, :] = q_h
        q_cols[:, r] = q_h.T

    lanes = max(2 * tokens, 256) if heads % 2 == 0 else tokens
    chunks = rows // lanes
    lane = lax.rem(lax.broadcasted_iota(jnp.int32, (1, lanes), 1), tokens)
    o0, o1 = order[me * 2], order[me * 2 + 1]
    query_pos = jnp.where(lane < span, o0 * span + lane, o1 * span + lane - span)
    key_row = lax.broadcasted_iota(jnp.int32, (2 * tokens, 1), 0)

    def allowed(to):
        key_pos = order[to * 4] * span + key_row
        for i in range(1, 4):
            key_pos = jnp.where(
                key_row >= i * span, order[to * 4 + i] * span + key_row - i * span, key_pos
            )
        return key_pos <= query_pos

    def pair_of(held, to):
        return held[pl.ds(to * 2, 2)].reshape(2 * tokens, head_dim)

    keep = scores.shape[0] == nz
    top[...] = jnp.full_like(top, big_negative)
    total[...] = jnp.zeros_like(total)

    def stats(j, carry):
        to = peer(j)
        kv_copy(0, to * 2 + other, kv_fwd.at[0, j], partner).wait_recv()
        mask = allowed(to)
        keys = pair_of(kk, to)
        for c in range(chunks):
            at = slice(c * lanes, (c + 1) * lanes)
            s = jnp.where(mask, dot(keys, q_cols[:, at]) * scale2, big_negative)
            if keep:
                scores[j, :, at] = s
            old = top[:, at]
            new = jnp.maximum(old, jnp.max(s, axis=0, keepdims=True))
            total[:, at] = total[:, at] * jnp.exp2(old - new) + jnp.sum(
                jnp.exp2(s - new), axis=0, keepdims=True
            )
            top[:, at] = new

        @pl.when(j + 1 < nz)
        def _():
            pass_on(1, j + 1, 0)

        return carry

    lax.fori_loop(0, nz, stats, 0)
    top[...] = top[...] + jnp.log(total[...]) * math.log2(math.e)
    dq_cols[...] = jnp.zeros_like(dq_cols)

    def to_partner(j):
        to = peer(j)
        return remote(
            part.at[to, other], from_partner.at[to], part_send.at[j], part_recv.at[j],
            "ctx", partner,
        )

    def to_owner(j):
        to = peer(j)
        return remote(
            z_out.at[j], z_in.at[j], z_send.at[j], z_recv.at[j], "ctx", to * 2 + side
        )

    def settle(j):
        to = peer(j)
        to_partner(j).wait_recv()
        both = part[to, side].astype(F32) + from_partner[to].astype(F32)
        z_out[j] = both.astype(BF16)
        to_owner(j).start()

    def grad(i, carry):
        j = lax.rem(i + 1, nz)
        to = peer(j)
        mask = None if keep else allowed(to)
        kv_copy(1, to * 2 + other, kv_fwd.at[1, j], partner).wait_recv()
        keys, values = pair_of(kk, to), pair_of(vv, to)
        for c in range(chunks):
            at = slice(c * lanes, (c + 1) * lanes)
            if keep:
                s = scores[j, :, at]
            else:
                s = jnp.where(mask, dot(keys, q_cols[:, at]) * scale2, big_negative)
            p = jnp.exp2(s - top[:, at])
            dp = dot(values, do_cols[:, at])
            p_b[:, at] = p.astype(BF16)
            ds_b[:, at] = (p * (dp - delta[:, at])).astype(BF16)
        @pl.when(i > 1)
        def _():
            settle(i - 1)

        dk = dot(ds_b[...], q_rows[...]) * scale
        dv = dot(p_b[...], do_rows[...])
        part[to, :, :, :head_dim] = dk.astype(BF16).reshape(2, tokens, head_dim)
        part[to, :, :, head_dim:] = dv.astype(BF16).reshape(2, tokens, head_dim)
        to_partner(j).start()
        dq_cols[...] += dot(keys.T, ds_b[...])

        return carry

    lax.fori_loop(0, nz, grad, 0)

    for h in range(heads):
        dq_b[h * head_dim:(h + 1) * head_dim, :] = (
            dq_cols[:, h * tokens:(h + 1) * tokens] * scale
        ).astype(BF16)
    tile = min(512, width)

    def query_terms(i, carry):
        at = pl.ds(pl.multiple_of(i * tile, tile), tile)
        grads[at, :] = dot(wq[at, :], dq_b[...])
        return carry

    early = 1
    lax.fori_loop(0, early, query_terms, 0)
    if nz > 1:
        settle(nz - 1)
    lax.fori_loop(early, width // tile, query_terms, 0)

    to_partner(0).wait_recv()
    mine = part[z, side].astype(F32) + from_partner[z].astype(F32)

    def gather_terms(j, acc):
        to_owner(j).wait_recv()
        return acc + z_in[j].astype(F32)

    mine = lax.fori_loop(1, nz, gather_terms, mine)
    dkv = mine.T.astype(BF16)

    size = features // pieces

    def rows_of(b, c, i):
        start = (lax.rem(pair + b, na) * 2 + c) * features + i * size
        return pl.ds(pl.multiple_of(start, size), size)

    def to_core(b, i):
        return remote(
            t_out.at[b, i], t_in.at[b, i], t_send.at[b, i], t_recv.at[b, i], "tp", t_partner
        )

    def across(b, i):
        to = lax.rem(pair + b, na) * 2 + core
        return remote(y_out.at[b, i], y_in.at[b, i], y_send.at[b, i], y_recv.at[b, i], "tp", to)

    for b in [b % na for b in range(1, na + 1)]:
        for i in range(pieces):
            at = rows_of(b, 1 - core, i)
            t_out[b, i] = (grads[at, :] + dot(wkv[at, :], dkv)).astype(BF16)
            to_core(b, i).start()
        for i in range(pieces):
            at = rows_of(b, core, i)
            term = grads[at, :] + dot(wkv[at, :], dkv)
            to_core(b, i).wait_recv()
            term = term + t_in[b, i].astype(F32)
            if b > 0:
                y_out[b, i] = term.astype(BF16)
                across(b, i).start()
            else:
                grads[at, :] = term
    for i in range(pieces):
        term = grads[rows_of(0, core, i), :]
        for b in range(1, na):
            across(b, i).wait_recv()
            term = term + y_in[b, i].astype(F32)
        out[:, i * size:(i + 1) * size] = term.T.astype(BF16)

    def drain(j, carry):
        forward(0, j).wait_send()
        forward(1, j).wait_send()
        to_partner(j).wait_send()
        return carry

    def drain_z(j, carry):
        kv_out(0, j).wait_send()
        kv_out(1, j).wait_send()
        to_owner(j).wait_send()
        return carry

    lax.fori_loop(0, nz, drain, 0)
    lax.fori_loop(1, nz, drain_z, 0)
    for b in range(na):
        for i in range(pieces):
            to_core(b, i).wait_send()
            if b > 0:
                across(b, i).wait_send()


def on_device(n, m, inputs, w_query, w_key, w_value, attn_out, d_out, block_order):
    tokens, width = inputs.shape
    head_dim = w_key.shape[1]
    local_width = w_query.shape[1]
    rows = local_width // head_dim * tokens
    features = width // m
    nz, na = n // 2, m // 2
    keep = n * tokens * rows * 4 <= kept_scores
    vmem, dma = pltpu.VMEM, pltpu.SemaphoreType.DMA
    block = (tokens, 2 * head_dim)
    scratch = [
        vmem((tokens, width), BF16),
        vmem((width, local_width), BF16),
        vmem((width, 2 * head_dim), BF16),
        vmem((tokens, local_width), BF16),
        vmem((tokens, local_width), BF16),
        vmem((tokens, local_width), F32),
        vmem((rows, head_dim), BF16),
        vmem((head_dim, rows), BF16),
        vmem((rows, head_dim), BF16),
        vmem((head_dim, rows), BF16),
        vmem((1, rows), F32),
        vmem((1, rows), F32),
        vmem((1, rows), F32),
        vmem((n, tokens, head_dim), BF16),
        vmem((n, tokens, head_dim), BF16),
        vmem((nz if keep else 1, 2 * tokens, rows), F32),
        vmem((2 * tokens, rows), BF16),
        vmem((2 * tokens, rows), BF16),
        vmem((head_dim, rows), F32),
        vmem((nz, 2, *block), BF16),
        vmem((nz, *block), BF16),
        vmem((nz, *block), BF16),
        vmem((nz, *block), BF16),
        vmem((local_width, tokens), BF16),
        vmem((width, tokens), F32),
        vmem((na, pieces, features // pieces, tokens), BF16),
        vmem((na, pieces, features // pieces, tokens), BF16),
        vmem((na, pieces, features // pieces, tokens), BF16),
        vmem((na, pieces, features // pieces, tokens), BF16),
        dma((4, q_chunks)), dma((2,)), dma((2, nz)), dma((2, nz)), dma((2, n)),
        dma((nz,)), dma((nz,)), dma((nz,)), dma((nz,)),
        dma((na, pieces)), dma((na, pieces)), dma((na, pieces)), dma((na, pieces)),
    ]
    seq = tokens * n
    flops = 2 * tokens * (2 * width * (local_width + 2 * head_dim) + 6 * seq * local_width)
    return pl.pallas_call(
        functools.partial(kernel, n, m),
        out_shape=pltpu.VMEM((tokens, features), BF16),
        in_specs=[pl.BlockSpec(memory_space=pltpu.SMEM)] + [pl.BlockSpec(memory_space=pl.ANY)] * 6,
        out_specs=pl.BlockSpec(memory_space=pltpu.VMEM),
        scratch_shapes=scratch,
        compiler_params=pltpu.CompilerParams(
            collective_id=0, has_side_effects=True, vmem_limit_bytes=58 * 2**20
        ),
        cost_estimate=pl.CostEstimate(
            flops=flops, bytes_accessed=2 * width * (local_width + 2 * head_dim + 2 * tokens),
            transcendentals=2 * rows * seq,
        ),
    )(block_order, inputs, w_query, w_key, w_value, attn_out, d_out)


def solution(mesh):
    placed = (
        P("ctx", None),
        P(None, "tp"),
        P(None, "tp"),
        P(None, "tp"),
        P("ctx", "tp"),
        P("ctx", "tp"),
        P(),
    )
    return jax.shard_map(
        functools.partial(on_device, mesh.shape["ctx"], mesh.shape["tp"]),
        mesh=mesh, in_specs=placed, out_specs=P("ctx", "tp"), check_vma=False,
    )
```
